32 devices in a mesh: section: 2 (over core), dp: 4 (over z), expert: 4 (over y, x).
Axes of the slice: x: 2, y: 2, z: 4, core: 2. Of those that a mesh axis runs over, the one named last changes fastest.
Arguments:
- inputs: bfloat16 [2, 4, 1024, 768], P(None, 'expert', 'dp'), may hold values from -6 to 6
- cotangent: bfloat16 [2, 4, 1024, 768], P(None, 'expert', 'dp'), may hold values from -6 to 6
- lengths: int32 [8, 3], replicated, may hold values from 1 to 896, 1024 in all within a row
- deal: int32 [8], replicated, may hold values from 0 to 7, each once
- routes: int32 [2, 4, 1024, 2], P(None, 'expert', 'dp'), may hold values from 0 to 3, all different within a row; in each aligned block of 256 rows (0 to 255, 256 to 511, ..., all dimensions but the last counted through in order) at most 192 rows name the same one
- order: int32 [2, 4, 2048], P(None, 'expert', 'dp'), may hold values from 0 to 511, as said below
- gains: bfloat16 [2, 2, 768], P('section', None, 'expert'), may hold values from 0.5 to 1.5
- w_qkv: bfloat16 [2, 768, 2304], P('section', 'expert'), may hold values from -0.21875 to 0.21875
- w_out: bfloat16 [2, 768, 768], P('section', 'expert'), may hold values from -1.75 to 1.75
- w_router: bfloat16 [2, 768, 4], P('section', 'expert'), may hold values from -0.21875 to 0.21875
- w_shared_in: bfloat16 [2, 768, 4096], P('section', 'expert'), may hold values from -0.21875 to 0.21875
- w_shared_down: bfloat16 [2, 2048, 768], P('section', 'expert'), may hold values from -0.125 to 0.125
- w_expert_in: bfloat16 [2, 4, 768, 4096], P('section', 'expert'), may hold values from -0.21875 to 0.21875
- w_expert_down: bfloat16 [2, 4, 2048, 768], P('section', 'expert'), may hold values from -0.125 to 0.125
Outputs:
- section_out: bfloat16 [2, 2, 4, 1024, 768], P('section', None, 'expert', 'dp')
- input_grad: float32 [2, 2, 4, 1024, 768], P('section', None, 'expert', 'dp')
- grad_gains: float32 [2, 2, 768], P('section', None, 'expert')
- grad_qkv: float32 [2, 768, 2304], P('section', 'expert')
- grad_out: float32 [2, 768, 768], P('section', 'expert')
- grad_router: float32 [2, 768, 4], P('section', 'expert')
- grad_shared_in: float32 [2, 768, 4096], P('section', 'expert')
- grad_shared_down: float32 [2, 2048, 768], P('section', 'expert')
- grad_expert_in: float32 [2, 4, 768, 4096], P('section', 'expert')
- grad_expert_down: float32 [2, 4, 2048, 768], P('section', 'expert')
The draws below stay inside these ranges and needn't reach their ends.
Inputs may be any that keep to these rules, and one draw needn't show every extreme that they name: Row r of lengths holds the lengths of 3 sequences laid end to end in a pack of 1024 tokens; the longest of each row is 896. A permutation; pack j of micro-batch m takes row deal[m * 4 + j] of lengths. `routes`: each token names two different experts; in each aligned block of 256 positions of a pack no expert is named more than 192 times. `order`: each aligned block of 512 entries (one block's pairs, token-major) is a permutation; a lower value is slotted first.
All inputs are finite; a program needn't handle non-finite values.
Results may differ from the reference program's by a relative error of at most 0.028.
Values may be sent and summed in bfloat16 or wider, within the bound.
No kernel may reach another device: no remote copies, remote signals or barrier semaphores. Data moves between devices by JAX's collectives and lax.ppermute only.
A program may use at most 320 MiB of HBM per device.

```python
import math
import jax
import jax.numpy as jnp
import numpy as np
from jax import lax

D = 768
HEADS = 12
HEAD = 64
FF = 2048
MB = 2
TOK_MB = 256
NSEQ = 3
EXPERTS = 4
PACKS_MB = 4
PACKS = 8
PACK = 1024
LONGEST = 896
SEND = 192
CAP = 512


def draw_order(key, part):
    key = jax.random.fold_in(key, 11)
    lanes = PACK // TOK_MB
    block_keys = jax.random.split(key, MB * PACKS_MB * lanes)
    shuffled = jax.vmap(lambda single: jax.random.permutation(single, 2 * TOK_MB))(block_keys)
    return shuffled.reshape(MB, PACKS_MB, 2 * PACK).astype(jnp.int32)


def steps_of(own_key, extent, cuts, low, largest):
    level = 1.0
    for dim, shards_of in cuts:
        draws = jax.random.uniform(jax.random.fold_in(jax.random.fold_in(own_key, 6), dim), (shards_of,), jnp.float32, low / len(cuts), largest / len(cuts))
        level = level * jnp.repeat(jnp.exp(draws), extent[dim] // shards_of).reshape((-1,) + (1,) * (len(extent) - 1 - dim))
    return level


def split_up(count, total, bound, lean):
    loads = [(1 << 20) // math.isqrt(standing ** lean) + 1 for standing in range(2, count + 1)]
    surplus, given = total - bound - (count - 1), [1] * (count - 1)
    while surplus > 0:
        candidates = [i for i in range(count - 1) if given[i] < bound]
        whole, budget = sum([loads[i] for i in candidates]), surplus
        for i in candidates:
            extra = min(bound - given[i], max(1, budget * loads[i] // whole), surplus)
            given[i] = given[i] + extra
            surplus = surplus - extra
    return np.array([bound] + given)


def ragged_sizes(key, count, total, bound, skew):
    if count == 2:
        one = jax.random.randint(key, (), max(1, total - bound), min(bound, total - 1) + 1)
        return jnp.stack([one, total - one])
    sizes = jnp.asarray(split_up(count, total, bound, skew), jnp.int32)
    couples = (count - 1) // 2
    source_of, sink = sizes[1:1 + 2 * couples:2], sizes[2:2 + 2 * couples:2]
    room = jnp.minimum(source_of - 1, bound - sink)
    moved = jax.random.randint(jax.random.fold_in(key, 1), (couples,), 0, 1 << 20) % (room + 1)
    sizes = sizes.at[1:1 + 2 * couples:2].set(source_of - moved).at[2:2 + 2 * couples:2].set(sink + moved)
    return sizes[jax.random.permutation(jax.random.fold_in(key, 2), count)]


def deal_out(stream_key, own, number, rows, number_of, top, most, lean):
    sequence = jax.random.permutation(stream_key, number_of)
    packed, common = load_shares(number_of, rows * top, most, lean, True), load_shares(number_of, rows * top, most, lean, False)
    places = jnp.arange(number_of)

    def named(sizes, rotation):
        used = int((sizes > 0).sum())
        fixed = max(1, used // 4)
        moved = fixed + (places - fixed + rotation * (used - fixed)) % max(1, number_of - fixed)
        return jnp.zeros((number_of,), jnp.int32).at[sequence[jnp.where(places < fixed, places, moved)]].set(jnp.asarray(sizes, jnp.int32))

    sizes = jnp.where(number % 4 == 0, named(packed, number // 4), named(common, number - number // 4 - 1))
    mixed = jax.random.permutation(jax.random.fold_in(own, 3), number_of)
    donor, sink = mixed[0:number_of // 2 * 2:2], mixed[1:number_of // 2 * 2:2]
    margin = jnp.minimum(sizes[donor] - 1, most - sizes[sink]) // 2
    margin = jnp.where((donor == sequence[0]) | (sink == sequence[0]) | (sizes[sink] == 0), 0, jnp.maximum(margin, 0))
    moved = jax.random.randint(jax.random.fold_in(own, 4), (number_of // 2,), 0, 1 << 20) % (margin + 1)
    sizes = sizes.at[donor].add(-moved).at[sink].add(moved)
    labels = jnp.searchsorted(jnp.cumsum(sizes), jnp.arange(rows * top), side="right").astype(jnp.int32)
    listing = labels.reshape(top, rows).T
    listing = listing[jax.random.permutation(jax.random.fold_in(own, 1), rows)]
    rotation = jax.random.randint(jax.random.fold_in(own, 2), (rows, 1), 0, top)
    return jnp.take_along_axis(listing, (jnp.arange(top)[None, :] + rotation) % top, axis=1)


def load_shares(count, total, limit, lean, full):
    portions = [(1 << 20) // math.isqrt(standing ** lean) + 1 for standing in range(1, count + 1)]
    largest = limit if full else min(limit, max(-(-total // count), total * portions[0] // sum(portions)))
    least = 1 if total - largest >= count - 1 else 0
    given, surplus = [largest] + [least] * (count - 1), total - largest - least * (count - 1)
    while surplus > 0:
        movable = [i for i in range(1, count) if given[i] < largest] or [i for i in range(1, count) if given[i] < limit]
        whole, left = sum([portions[i] for i in movable]), surplus
        for i in movable:
            addition = min(limit - given[i], max(1, left * portions[i] // whole), surplus)
            given[i] = given[i] + addition
            surplus = surplus - addition
    return np.array(given)


def centred(stream_key, extent, deviation, bound, cuts=(), kind=jnp.bfloat16):
    array = deviation * jax.random.normal(stream_key, extent, jnp.float32)
    if cuts:
        array = array * steps_of(stream_key, extent, cuts, -0.22, 0.18)
    return jnp.clip(array, -bound, bound).astype(kind)


def setup_inputs(seed: int = 0) -> dict:
    splits = jax.random.split(jax.random.key(seed), 15)
    inputs = centred(splits[0], (MB, PACKS_MB, PACK, D), 1.0, 6.0, ((1, 4), (2, 4)))
    cotangent = centred(splits[1], (MB, PACKS_MB, PACK, D), 1.0, 6.0, ((1, 4), (2, 4)))
    lengths = jax.vmap(lambda own: ragged_sizes(own, NSEQ, PACK, LONGEST, 2))(jax.random.split(splits[2], PACKS)).reshape((PACKS, NSEQ)).astype(jnp.int32)
    deal = jax.random.permutation(splits[3], PACKS).astype(jnp.int32)
    routes_keys = jax.random.split(jax.random.fold_in(splits[4], 1), MB * PACKS_MB * PACK // TOK_MB)
    routes_turns = jax.random.permutation(jax.random.fold_in(splits[4], 3), MB * PACKS_MB * PACK // TOK_MB)
    routes = jax.vmap(lambda own, number: deal_out(jax.random.fold_in(splits[4], 2), own, number, TOK_MB, EXPERTS, 2, SEND, 2))(routes_keys, routes_turns).reshape((MB, PACKS_MB, PACK, 2))
    order = draw_order(jax.random.fold_in(splits[14], 71), 0)
    gains = jnp.clip(1.0 + 0.1 * jax.random.normal(splits[6], (2, 2, D), jnp.float32), 0.5, 1.5).astype(jnp.bfloat16)
    w_qkv = centred(splits[7], (2, D, 3 * D), D ** -0.5, 0.21875, ((0, 2), (1, 4)))
    w_out = centred(splits[8], (2, D, D), (D // 64) ** -0.5, 1.75, ((0, 2), (1, 4)))
    w_router = centred(splits[9], (2, D, EXPERTS), D ** -0.5, 0.21875, ((0, 2), (1, 4)))
    w_shared_in = centred(splits[10], (2, D, 2 * FF), D ** -0.5, 0.21875, ((0, 2), (1, 4)))
    w_shared_down = centred(splits[11], (2, FF, D), FF ** -0.5, 0.125, ((0, 2), (1, 4)))
    w_expert_in = centred(splits[12], (2, EXPERTS, D, 2 * FF), D ** -0.5, 0.21875, ((0, 2), (1, 4)))
    w_expert_down = centred(splits[13], (2, EXPERTS, FF, D), FF ** -0.5, 0.125, ((0, 2), (1, 4)))
    return dict(inputs=inputs, cotangent=cotangent, lengths=lengths, deal=deal, routes=routes, order=order, gains=gains, w_qkv=w_qkv, w_out=w_out, w_router=w_router, w_shared_in=w_shared_in, w_shared_down=w_shared_down, w_expert_in=w_expert_in, w_expert_down=w_expert_down)


@jax.custom_vjp
def low(v):
    return lax.optimization_barrier(v.astype(jnp.bfloat16)).astype(jnp.float32)

@jax.custom_vjp
def low_back(v):
    return v

def low_keep(v):
    return (low(v), None)

def low_pass(kept, grad):
    return (grad,)

def back_keep(v):
    return (v, None)

def back_low(kept, grad):
    return (low(grad),)
low.defvjp(low_keep, low_pass)
low_back.defvjp(back_keep, back_low)
highest = lax.Precision.HIGHEST
epsilon = 1e-06

def norm_scale(values, gain):
    return values * lax.rsqrt(lax.optimization_barrier(jnp.mean(values * values, axis=-1, keepdims=True)) + epsilon) * gain

def softmax_last(values):
    shifted = values - lax.optimization_barrier(jnp.max(values, axis=-1, keepdims=True))
    raised = jnp.exp(shifted)
    return raised / lax.optimization_barrier(jnp.sum(raised, axis=-1, keepdims=True))

def pack_attention(query, key_heads, value_heads, segment_of):
    block = min(512, PACK)
    places = jnp.arange(PACK, dtype=jnp.int32)
    score_scale = HEAD ** (-0.5)

    def one_block(start):
        query_block = lax.dynamic_slice_in_dim(query, start, block, 0)
        segment_block = lax.dynamic_slice_in_dim(segment_of, start, block, 0)
        rows_here = start + jnp.arange(block, dtype=jnp.int32)
        scores = low_back(score_scale * jnp.einsum('qhd,khd->hqk', query_block, key_heads, precision=highest))
        allowed = (places[None, :] <= rows_here[:, None]) & (segment_of[None, :] == segment_block[:, None])
        scores = jnp.where(allowed[None], scores, -1e+30)
        weights = low(softmax_last(scores))
        return jnp.einsum('hqk,khd->qhd', weights, value_heads, precision=highest)
    starts = jnp.arange(PACK // block, dtype=jnp.int32) * block
    return lax.map(jax.checkpoint(one_block), starts).reshape(PACK, HEADS, HEAD)

def group_experts(hidden, gates, routes_here, order_here, w_in, w_down):
    packs = hidden.shape[0]
    pair_expert = routes_here.reshape(packs, 2 * TOK_MB)
    pair_order = order_here.reshape(packs, 2 * TOK_MB)
    same_expert = pair_expert[:, :, None] == pair_expert[:, None, :]
    earlier = pair_order[:, None, :] < pair_order[:, :, None]
    slot_rank = lax.optimization_barrier(jnp.sum(same_expert & earlier, axis=2)).astype(jnp.int32)
    onehot = (pair_expert[..., None] == jnp.arange(EXPERTS, dtype=jnp.int32)).astype(jnp.int32)
    counts = lax.optimization_barrier(jnp.sum(onehot, axis=1)).astype(jnp.int32)
    before = (jnp.cumsum(counts, axis=0) - counts).astype(jnp.int32)
    global_slot = lax.optimization_barrier(jnp.sum(onehot * before[:, None, :], axis=2)).astype(jnp.int32) + slot_rank
    kept_mask = global_slot < CAP
    target = jnp.where(kept_mask, pair_expert * CAP + global_slot, EXPERTS * CAP).reshape(-1).astype(jnp.int32)
    copies = low_back(jnp.repeat(hidden, 2, axis=1)).reshape(-1, D)
    buffer = jnp.zeros((EXPERTS * CAP + 1, D), jnp.float32).at[target].add(copies)
    buffer = buffer[:EXPERTS * CAP].reshape(EXPERTS, CAP, D)
    expert_pre = low_back(jnp.einsum('ecd,edf->ecf', buffer, w_in, precision=highest))
    expert_act = low(jax.nn.silu(expert_pre[..., :FF]) * expert_pre[..., FF:])
    expert_res = low_back(low(jnp.einsum('ecf,efd->ecd', expert_act, w_down, precision=highest)))
    padded = jnp.concatenate([expert_res.reshape(EXPERTS * CAP, D), jnp.zeros((1, D), jnp.float32)], axis=0)
    pair_values = padded[target].reshape(packs, TOK_MB, 2, D)
    pair_weight = gates * kept_mask.reshape(packs, TOK_MB, 2).astype(jnp.float32)
    return lax.optimization_barrier(jnp.sum(pair_weight[..., None] * pair_values, axis=2))

def all_groups(hidden_two, gate_values, routes_now, order_now, w_expert_in, w_expert_down):
    packs = hidden_two.shape[0]
    lanes = PACK // TOK_MB

    def split_rows(values):
        return jnp.swapaxes(values.reshape((packs, lanes, TOK_MB) + values.shape[2:]), 0, 1)
    grouped = (split_rows(hidden_two), split_rows(gate_values), split_rows(routes_now), split_rows(order_now.reshape(packs, PACK, 2)))
    results = lax.map(lambda parts: group_experts(parts[0], parts[1], parts[2], parts[3], w_expert_in, w_expert_down), grouped)
    return jnp.swapaxes(results, 0, 1).reshape(packs, PACK, D)

def section_layer(weights, inputs_now, segment_of, routes_now, order_now):
    gains, w_qkv, w_out, w_router, w_shared_in, w_shared_down, w_expert_in, w_expert_down = weights
    packs = inputs_now.shape[0]
    hidden_one = low(norm_scale(inputs_now, gains[0]))
    projected = jnp.einsum('pnd,de->pne', hidden_one, w_qkv, precision=highest)
    query = low_back(low(projected[..., :D])).reshape(packs, PACK, HEADS, HEAD)
    key_heads = low_back(low(projected[..., D:2 * D])).reshape(packs, PACK, HEADS, HEAD)
    value_heads = low_back(low(projected[..., 2 * D:])).reshape(packs, PACK, HEADS, HEAD)
    mixed = lax.map(lambda parts: pack_attention(parts[0], parts[1], parts[2], parts[3]), (query, key_heads, value_heads, segment_of))
    mixed = low_back(low(mixed.reshape(packs, PACK, D)))
    middle = inputs_now + low_back(jnp.einsum('pnd,de->pne', mixed, w_out, precision=highest))
    hidden_two = low(norm_scale(middle, gains[1]))
    logits = low_back(jnp.einsum('pnd,de->pne', hidden_two, w_router, precision=highest))
    router_probs = softmax_last(logits)
    chosen = (routes_now[..., None] == jnp.arange(EXPERTS, dtype=jnp.int32)).astype(jnp.float32)
    picked = lax.optimization_barrier(jnp.sum(router_probs[:, :, None, :] * chosen, axis=-1))
    gate_values = picked / lax.optimization_barrier(jnp.sum(picked, axis=-1, keepdims=True))
    shared_pre = low_back(jnp.einsum('pnd,df->pnf', hidden_two, w_shared_in, precision=highest))
    shared_act = low(jax.nn.silu(shared_pre[..., :FF]) * shared_pre[..., FF:])
    shared_out = low_back(jnp.einsum('pnf,fd->pnd', shared_act, w_shared_down, precision=highest))
    expert_out = all_groups(hidden_two, gate_values, routes_now, order_now, w_expert_in, w_expert_down)
    return middle + shared_out + expert_out

def reference(inputs, cotangent, lengths, deal, routes, order, gains, w_qkv, w_out, w_router, w_shared_in, w_shared_down, w_expert_in, w_expert_down):
    pack_lengths = jnp.take(lengths, deal, axis=0).reshape(MB, PACKS_MB, NSEQ)
    pack_ends = jnp.cumsum(pack_lengths, axis=-1)
    places = jnp.arange(PACK, dtype=jnp.int32)
    segments = lax.optimization_barrier(jnp.sum(places[None, None, :, None] >= pack_ends[:, :, None, :], axis=-1)).astype(jnp.int32)
    stacked = (gains, w_qkv, w_out, w_router, w_shared_in, w_shared_down, w_expert_in, w_expert_down)

    def section_params(index):
        return tuple((weight[index].astype(jnp.float32) for weight in stacked))

    def section_run(params, values):
        return jnp.stack([section_layer(params, values[batch_index], segments[batch_index], routes[batch_index], order[batch_index]) for batch_index in range(MB)])
    first_out, first_pull = jax.vjp(section_run, section_params(0), inputs.astype(jnp.float32))
    handed = first_out.astype(jnp.bfloat16)
    second_out, second_pull = jax.vjp(section_run, section_params(1), handed.astype(jnp.float32))
    second_grads, second_input = second_pull(cotangent.astype(jnp.float32))
    first_grads, first_input = first_pull(low(second_input))
    section_out = jnp.stack([handed, second_out.astype(jnp.bfloat16)])
    input_grad = jnp.stack([first_input, second_input])
    joined = [jnp.stack([first_grads[index], second_grads[index]]) for index in range(8)]
    return (section_out, input_grad, joined[0], joined[1], joined[2], joined[3], joined[4], joined[5], joined[6], joined[7])
```

```python
import functools
import jax
import jax.numpy as jnp
from jax import lax
from jax.experimental import pallas as pl
from jax.experimental.pallas import tpu as pltpu
from jax.sharding import PartitionSpec as P

HEADS = 12
HEAD = 64
FF = 2048
EPS = 1e-06

SEC, DP, EXP = "section", "dp", "expert"
BF, F32, I32 = jnp.bfloat16, jnp.float32, jnp.int32
SWAP = [(0, 1), (1, 0)]


def mm(a, b, ca=1, cb=0, out=F32):
    r = lax.dot_general(a, b, (((ca,), (cb,)), ((), ())), preferred_element_type=F32)
    return r.astype(out)


def swap_cores(v):
    return lax.ppermute(v, SEC, SWAP)


def a2a(v, axis):
    return lax.all_to_all(v, axis, split_axis=0, concat_axis=0, tiled=True)


def gather(v, axis):
    return lax.all_gather(v, axis, axis=0, tiled=True)


def xor_pairs(count, k):
    return [(i, i ^ k) for i in range(count)]


def gather_blocks(v, members):
    return [v] + [lax.ppermute(v, EXP, xor_pairs(members, k)) for k in range(1, members)]


def scatter_blocks(blocks):
    count = len(blocks)
    return [blocks[0]] + [lax.ppermute(blocks[k], EXP, xor_pairs(count, k)) for k in range(1, count)]


def half_of(v, which, axis=0):
    size = v.shape[axis] // 2
    return lax.dynamic_slice_in_dim(v, which * size, size, axis)


def by_core(core, first, second):
    return jnp.where(core == 0, first, second)


def norm_apply(values, gain):
    scale = lax.rsqrt(jnp.mean(values * values, axis=-1, keepdims=True) + EPS)
    return (values * scale * gain).astype(BF), scale


def norm_backward(grad_hidden, values, scale, gain):
    normed = values * scale
    grad_gain = jnp.sum(grad_hidden * normed, axis=0)
    grad_normed = grad_hidden * gain
    grad_values = scale * (
        grad_normed - normed * jnp.mean(grad_normed * normed, axis=-1, keepdims=True)
    )
    return grad_values, grad_gain


def silu(v):
    return v * jax.nn.sigmoid(v)


def silu_parts(v):
    logistic = jax.nn.sigmoid(v)
    return v * logistic, logistic * (1.0 + v * (1.0 - logistic))


def block_mask(ends_ref, first_row, rows, cols):
    q = first_row + lax.broadcasted_iota(I32, (rows, cols), 0)
    k = lax.broadcasted_iota(I32, (rows, cols), 1)
    start = jnp.zeros((rows, cols), I32)
    for i in range(ends_ref.shape[0]):
        end = ends_ref[i]
        start = jnp.where(q >= end, end, start)
    return (k <= q) & (k >= start)


def head_slices(ref, rows, head, per, parts):
    return [ref[rows, (part * per + head) * HEAD : (part * per + head + 1) * HEAD] for part in parts]


def block_probs(q, k, mask):
    scores = lax.dot_general(q, k, (((1,), (1,)), ((), ())), preferred_element_type=F32)
    scores = jnp.where(mask, scores * (HEAD**-0.5), -1e30)
    raised = jnp.exp(scores - jnp.max(scores, axis=-1, keepdims=True))
    return raised / jnp.sum(raised, axis=-1, keepdims=True)


def attention_forward_kernel(block, per, ends_ref, qkv_ref, out_ref):
    pack = qkv_ref.shape[0]
    for i in range(pack // block):
        rows, reach = slice(i * block, (i + 1) * block), slice(0, (i + 1) * block)
        mask = block_mask(ends_ref, i * block, block, (i + 1) * block)
        for head in range(per):
            (q,) = head_slices(qkv_ref, rows, head, per, (0,))
            k, v = head_slices(qkv_ref, reach, head, per, (1, 2))
            probs = block_probs(q, k, mask).astype(BF)
            mixed = jnp.dot(probs, v, preferred_element_type=F32)
            out_ref[rows, head * HEAD : (head + 1) * HEAD] = mixed.astype(BF)


def attention_backward_kernel(block, per, ends_ref, qkv_ref, grad_ref, out_ref, dk_ref, dv_ref):
    pack = qkv_ref.shape[0]
    dk_ref[...] = jnp.zeros_like(dk_ref)
    dv_ref[...] = jnp.zeros_like(dv_ref)
    for i in range(pack // block):
        rows, reach = slice(i * block, (i + 1) * block), slice(0, (i + 1) * block)
        mask = block_mask(ends_ref, i * block, block, (i + 1) * block)
        for head in range(per):
            (q,) = head_slices(qkv_ref, rows, head, per, (0,))
            k, v = head_slices(qkv_ref, reach, head, per, (1, 2))
            grad = grad_ref[rows, head * HEAD : (head + 1) * HEAD]
            probs = block_probs(q, k, mask)
            dprobs = lax.dot_general(grad, v, (((1,), (1,)), ((), ())), preferred_element_type=F32)
            delta = jnp.sum(probs * dprobs, axis=-1, keepdims=True)
            dscores = (probs * (dprobs - delta)).astype(BF)
            dq = jnp.dot(dscores, k, preferred_element_type=F32) * (HEAD**-0.5)
            out_ref[rows, head * HEAD : (head + 1) * HEAD] = dq.astype(BF)
            over_queries = (((0,), (0,)), ((), ()))
            dk_ref[head, reach, :] += lax.dot_general(
                dscores, q, over_queries, preferred_element_type=F32
            )
            dv_ref[head, reach, :] += lax.dot_general(
                probs.astype(BF), grad, over_queries, preferred_element_type=F32
            )
    for head in range(per):
        at = (per + head) * HEAD
        out_ref[:, at : at + HEAD] = (dk_ref[head] * (HEAD**-0.5)).astype(BF)
        at = (2 * per + head) * HEAD
        out_ref[:, at : at + HEAD] = dv_ref[head].astype(BF)


def vmem():
    return pl.BlockSpec(memory_space=pltpu.VMEM)


def attention_forward(ends, qkv, block):
    pack, columns = qkv.shape
    per = columns // (3 * HEAD)
    return pl.pallas_call(
        functools.partial(attention_forward_kernel, block, per),
        out_shape=jax.ShapeDtypeStruct((pack, per * HEAD), BF),
        in_specs=[pl.BlockSpec(memory_space=pltpu.SMEM), vmem()],
        out_specs=vmem(),
        compiler_params=pltpu.CompilerParams(vmem_limit_bytes=32 << 20),
        cost_estimate=pl.CostEstimate(
            flops=4 * per * pack * pack * HEAD, bytes_accessed=8 * pack * columns // 3, transcendentals=per * pack * pack
        ),
    )(ends, qkv)


def attention_backward(ends, qkv, grad, block):
    pack, columns = qkv.shape
    per = columns // (3 * HEAD)
    return pl.pallas_call(
        functools.partial(attention_backward_kernel, block, per),
        out_shape=jax.ShapeDtypeStruct((pack, columns), BF),
        in_specs=[pl.BlockSpec(memory_space=pltpu.SMEM), vmem(), vmem()],
        out_specs=vmem(),
        scratch_shapes=[pltpu.VMEM((per, pack, HEAD), F32)] * 2,
        compiler_params=pltpu.CompilerParams(vmem_limit_bytes=32 << 20),
        cost_estimate=pl.CostEstimate(
            flops=10 * per * pack * pack * HEAD, bytes_accessed=16 * pack * columns // 3, transcendentals=per * pack * pack
        ),
    )(ends, qkv, grad)


def section_weights(core, members, parts):
    gains, w_qkv, w_out, w_router, w_shared_in, w_shared_down, w_expert_in, w_expert_down = parts

    def both(mine):
        other = swap_cores(mine)
        return by_core(core, mine, other), by_core(core, other, mine)

    me = lax.axis_index(EXP)

    def shares(shard):
        mine, theirs = half_of(shard, core), half_of(shard, 1 - core)
        other = swap_cores(theirs)
        return by_core(core, mine, other), by_core(core, other, mine)

    def both_halves(full):
        blocks, rows, columns = full.shape
        other = swap_cores(full)
        halves = [by_core(core, full, other), by_core(core, other, full)]
        return jnp.stack(halves, axis=1).reshape(blocks * 2 * rows, columns)

    def permuted(part):
        blocks = jnp.stack(gather_blocks(part, members))
        return jnp.concatenate(
            [lax.dynamic_slice_in_dim(blocks, me ^ j, 1, 0) for j in range(members)]
        )

    rows, width = w_out.shape
    experts = w_router.shape[1]
    extra = experts + 2
    pad = -(-extra // 128) * 128 - extra
    small = jnp.concatenate([w_router, gains.T, jnp.zeros((rows, pad), BF)], axis=1)
    qkv_0, qkv_1 = shares(w_qkv)
    rest_0, rest_1 = shares(jnp.concatenate([w_out, small], axis=1))
    qkv_0 = both_halves(permuted(qkv_0))
    rest_0, _ = lax.optimization_barrier((rest_0, qkv_0))
    rest_0 = both_halves(permuted(rest_0))
    later, _ = lax.optimization_barrier((jnp.concatenate([qkv_1, rest_1], axis=1), qkv_0))
    dense_1 = both_halves(lax.all_gather(later, EXP))
    qkv = (qkv_0, dense_1[:, : 3 * width])
    rest = (rest_0, dense_1[:, 3 * width :])
    quarter = FF // members
    split = w_shared_in.reshape(rows, 2, members, quarter).transpose(2, 0, 1, 3)
    split = split.reshape(members, rows, 2 * quarter)
    shared_in = both(a2a(split, EXP).reshape(members * rows, 2 * quarter))
    shared_down = both(w_shared_down)
    expert_in = both(w_expert_in)
    expert_down = both(w_expert_down)
    return [
        (
            rest[s][:, width + experts : width + experts + 2].T.astype(F32),
            qkv[s],
            rest[s][:, :width],
            rest[s][:, width : width + experts],
            shared_in[s],
            shared_down[s],
            expert_in[s],
            expert_down[s],
        )
        for s in range(2)
    ]


def to_heads(v, lanes, parts):
    tokens, columns = v.shape
    per = columns // (parts * lanes)
    split = v.reshape(tokens, parts, lanes, per).transpose(2, 0, 1, 3).reshape(lanes, tokens, parts * per)
    return a2a(split, DP).reshape(lanes * tokens, parts * per)


def to_tokens(v, lanes, parts):
    pack, columns = v.shape
    tokens, per = pack // lanes, columns // parts
    got = a2a(v.reshape(lanes, tokens, columns), DP).reshape(lanes, tokens, parts, per)
    return got.transpose(1, 2, 0, 3).reshape(tokens, lanes * columns)


def layer_forward(current, context, weights):
    ends, chosen_all, slots, lanes, members, block = context
    gain, w_qkv, w_out, w_router, w_sin, w_sdown, w_ein, w_edown = weights
    tokens, width = current.shape
    hidden_one, scale_one = norm_apply(current, gain[0])
    qkv_heads = to_heads(mm(hidden_one, w_qkv, out=BF), lanes, 3)
    mixed = to_tokens(attention_forward(ends, qkv_heads, block), lanes, 1)
    middle = current + mm(mixed, w_out)
    hidden_two, scale_two = norm_apply(middle, gain[1])
    hidden_all = jnp.concatenate(gather_blocks(hidden_two, members))
    logits = mm(hidden_all, w_router)
    raised = jnp.exp(logits - jnp.max(logits, axis=-1, keepdims=True))
    router = raised / jnp.sum(raised, axis=-1, keepdims=True)
    both_picked = jnp.sum(router * chosen_all, axis=-1, keepdims=True)
    me = lax.axis_index(EXP)
    gate_here = lax.dynamic_slice_in_dim(router, me, 1, 1) / both_picked
    rows = mm(slots, hidden_all, out=BF)
    pre, act = branch(rows, w_ein, FF)
    result = mm(act, w_edown, out=BF)
    quarter = w_sdown.shape[0]
    shared_pre, shared_act = branch(hidden_all, w_sin, quarter)
    returned = mm(slots, result, 0, 0)
    partial = (gate_here * returned + mm(shared_act, w_sdown)).astype(BF)
    parts = scatter_blocks([partial[k * tokens : (k + 1) * tokens] for k in range(members)])
    output = middle + functools.reduce(jnp.add, [part.astype(F32) for part in parts])
    saved = (
        current, scale_one, hidden_one, qkv_heads, mixed, middle, scale_two, hidden_two, hidden_all,
        router, both_picked, gate_here, rows, pre, act, returned.astype(BF), shared_pre, shared_act,
    )
    return output, saved


def branch(rows, w_in, units):
    gate, up = mm(rows, w_in[:, :units], out=BF), mm(rows, w_in[:, units:], out=BF)
    return (gate, up), (silu(gate.astype(F32)) * up.astype(F32)).astype(BF)


def silu_grads(pre, grad_act):
    up = pre[1].astype(F32)
    value, slope = silu_parts(pre[0].astype(F32))
    return jnp.concatenate([grad_act * up * slope, grad_act * value], axis=1).astype(BF)


def layer_backward(grad_low, saved, context, weights):
    ends, chosen_all, slots, lanes, members, block = context
    gain, w_qkv, w_out, w_router, w_sin, w_sdown, w_ein, w_edown = weights
    (
        current, scale_one, hidden_one, qkv_heads, mixed, middle, scale_two, hidden_two, hidden_all,
        router_all, picked_all, gate_here, rows, pre, act, returned, shared_pre, shared_act,
    ) = saved
    tokens, width = current.shape
    core, me = lax.axis_index(SEC), lax.axis_index(EXP)
    grad_out = grad_low.astype(F32)
    grad_all = jnp.concatenate(gather_blocks(grad_low, members))
    wide = grad_all.astype(F32)
    dy = mm(slots, (gate_here * wide).astype(BF), out=BF)
    dgate = jnp.sum(wide * returned.astype(F32), axis=-1)
    dpre = silu_grads(pre, mm(dy, w_edown, 1, 1))
    drows = mm(dpre, w_ein, 1, 1, out=BF)
    dshared = silu_grads(shared_pre, mm(grad_all, w_sdown, 1, 1))
    partial = (mm(slots, drows, 0, 0) + mm(dshared, w_sin, 1, 1)).astype(BF)
    high = dgate.astype(BF)
    low = (dgate - high.astype(F32)).astype(BF)
    lines = -(-2 * tokens // (16 * width)) * 16
    blocks = []
    for k in range(members):
        own = slice(k * tokens, (k + 1) * tokens)
        pair = jnp.pad(jnp.concatenate([high[own], low[own]]), (0, lines * width - 2 * tokens))
        blocks.append(jnp.concatenate([partial[own], pair.reshape(lines, width)]))
    parts = scatter_blocks(blocks)
    dh2 = functools.reduce(jnp.add, [part[:tokens].astype(F32) for part in parts])
    gates = jnp.stack([part[tokens:].reshape(-1)[: 2 * tokens].astype(F32) for part in parts])
    gates = gates[:, :tokens] + gates[:, tokens:]
    column = jnp.arange(members, dtype=I32)[None, :]
    dgates = sum(
        jnp.where(column == (me ^ k), gates[k][:, None], 0.0) for k in range(members)
    )
    router, chosen, picked = router_all[:tokens], chosen_all[:tokens], picked_all[:tokens]
    inner = jnp.sum(dgates * router * chosen, axis=-1, keepdims=True) / picked
    dprob = chosen * (dgates - inner) / picked
    dlogits = (router * (dprob - jnp.sum(router * dprob, axis=-1, keepdims=True))).astype(BF)
    dh2 = dh2 + mm(dlogits, w_router, 1, 1)
    dmiddle_norm, dgain_two = norm_backward(dh2, middle, scale_two, gain[1])
    dmiddle = grad_out + dmiddle_norm
    dattn = dmiddle.astype(BF)
    dmixed = to_heads(mm(dattn, w_out, 1, 1, out=BF), lanes, 1)
    dqkv = to_tokens(attention_backward(ends, qkv_heads, dmixed, block), lanes, 3)
    dh1 = mm(dqkv, w_qkv, 1, 1)
    dinput_norm, dgain_one = norm_backward(dh1, current, scale_one, gain[0])
    grad_input = dmiddle + dinput_norm

    def halves(rows_of, grads):
        send = mm(half_of(rows_of, 1 - core, 1), grads, 0, 0, out=BF)
        keep = mm(half_of(rows_of, core, 1), grads, 0, 0)
        return (keep + swap_cores(send).astype(F32)).astype(BF)

    def halves_by_member(rows_of, grads):
        split = rows_of.reshape(rows_of.shape[0], members, 2, -1)

        def side(which):
            return lax.dynamic_index_in_dim(split, which, 2, False).reshape(rows_of.shape[0], -1)

        send = mm(side(1 - core), grads, 0, 0, out=BF)
        keep = mm(side(core), grads, 0, 0)
        return (keep + swap_cores(send).astype(F32)).astype(BF).reshape(members, -1, grads.shape[1])

    def small_halves(grad):
        split = grad.reshape(members, 2, -1, grad.shape[1])
        send = lax.dynamic_index_in_dim(split, 1 - core, 1, False).astype(BF)
        keep = lax.dynamic_index_in_dim(split, core, 1, False)
        return (keep + swap_cores(send).astype(F32)).astype(BF)

    def summed(parts):
        return jnp.sum(a2a(parts, EXP).astype(F32), axis=0).astype(BF)

    g_down = halves(act, dy)
    g_in = halves(rows, dpre)
    g_sdown = halves(shared_act, grad_all)
    g_sin = a2a(halves_by_member(hidden_all, dshared), EXP)
    extra = w_router.shape[1] + 2
    pad = -(-extra // 128) * 128 - extra
    small = jnp.concatenate(
        [
            mm(hidden_two, dlogits, 0, 0),
            jnp.stack([dgain_one, dgain_two], axis=1),
            jnp.zeros((width, pad), F32),
        ],
        axis=1,
    )
    g_out = halves_by_member(mixed, dattn)
    g_dense = summed(
        jnp.concatenate([halves_by_member(hidden_one, dqkv), g_out, small_halves(small)], axis=2)
    )
    return grad_input, (g_down, g_in, g_sdown, g_sin, g_dense)


def over_lanes(chunks):
    lane = lax.axis_index(DP)
    middle = (lane == 1) | (lane == 2)

    def add(a, b):
        return (a.astype(F32) + b.astype(F32)).astype(BF)

    arrived, result = [], []
    for k, chunk in enumerate(chunks):
        if k >= 2:
            chunk, _ = lax.optimization_barrier((chunk, arrived[k - 2]))
        arrived.append(lax.ppermute(chunk, DP, [(0, 1), (3, 2)]))
        part = add(chunk, arrived[k])
        total = add(part, lax.ppermute(part, DP, [(1, 2), (2, 1)]))
        result.append(jnp.where(middle, total, lax.ppermute(total, DP, [(1, 0), (2, 3)])))
    return result


def lane_sums(groups):
    done, last = [], None
    for group in groups:
        if last is not None:
            group, _ = lax.optimization_barrier((group, last))
        sums = lax.psum(tuple(group), DP)
        last = sums[0]
        done.append(tuple(sums))
    return done[0] + done[1], done[2] + done[3]


def local(
    inputs, cotangent, lengths, deal, routes, order, gains, w_qkv, w_out, w_router, w_shared_in, w_shared_down,
    w_expert_in, w_expert_down,
):
    core, me, lane = lax.axis_index(SEC), lax.axis_index(EXP), lax.axis_index(DP)
    members, lanes = lax.axis_size(EXP), lax.axis_size(DP)
    batches, _, tokens, width = inputs.shape
    experts = w_router.shape[2]
    assert batches == lax.axis_size(SEC) == 2 and w_expert_in.shape[1] == 1 and experts == members
    weights = section_weights(
        core,
        members,
        (
            gains[0], w_qkv[0], w_out[0], w_router[0], w_shared_in[0], w_shared_down[0],
            w_expert_in[0, 0], w_expert_down[0, 0],
        ),
    )
    row = lax.dynamic_index_in_dim(deal, core * members + me, 0, False)
    ends = jnp.cumsum(lax.dynamic_index_in_dim(lengths, row, 0, False))[:-1].astype(I32)
    pairs = lax.dynamic_index_in_dim(routes[:, 0], core, 0, False).reshape(-1)
    places = lax.dynamic_index_in_dim(order[:, 0], core, 0, False)
    same = pairs[:, None] == pairs[None, :]
    rank = jnp.sum((same & (places[None, :] < places[:, None])).astype(I32), axis=1)
    code = jnp.stack(gather_blocks(pairs * (2 * tokens) + rank, members))
    owner = me ^ jnp.arange(members, dtype=I32)
    pairs_all, rank_all = code // (2 * tokens), code % (2 * tokens)
    onehot = (pairs_all[:, :, None] == jnp.arange(experts, dtype=I32)).astype(I32)
    counts = jnp.sum(onehot, axis=1)
    lower = (owner[None, :] < owner[:, None]).astype(I32)
    before = jnp.sum(lower[:, :, None] * counts[None], axis=1)
    place = jnp.sum(onehot * before[:, None, :], axis=2) + rank_all
    capacity = 2 * tokens * members // experts
    slot = jnp.where((pairs_all == me) & (place < capacity), place, -1)
    slot = jnp.max(slot.reshape(members * tokens, 2), axis=1)
    slots = (jnp.arange(capacity, dtype=I32)[:, None] == slot[None, :]).astype(BF)
    chosen_all = jnp.sum(onehot.reshape(members * tokens, 2, experts), axis=1).astype(F32)
    context = (ends, chosen_all, slots, lanes, members, tokens)

    first_low = lax.dynamic_index_in_dim(inputs[:, 0], core, 0, False)
    grad_low = lax.dynamic_index_in_dim(cotangent[:, 0], core, 0, False)
    out_0, saved_0 = layer_forward(first_low.astype(F32), context, weights[0])
    low_0 = out_0.astype(BF)
    out_1, saved_1 = layer_forward(low_0.astype(F32), context, weights[1])
    low_1 = out_1.astype(BF)
    grad_1, terms_1 = layer_backward(grad_low, saved_1, context, weights[1])
    grad_0, terms_0 = layer_backward(grad_1.astype(BF), saved_0, context, weights[0])
    sum_1, sum_0 = lane_sums([terms_1[:2], terms_1[2:], terms_0[:2], terms_0[2:]])

    def to_section(of_0, of_1):
        mine = by_core(core, of_0, of_1)
        other = swap_cores(by_core(core, of_1, of_0))
        both = jnp.stack([by_core(core, mine, other), by_core(core, other, mine)])
        return both[None, :, None]

    def whole(half_0, half_1):
        got_1 = lax.ppermute(half_1, SEC, [(0, 1)])
        got_0 = lax.ppermute(half_0, SEC, [(1, 0)])
        return by_core(core, half_0, got_1).astype(F32), by_core(core, got_0, half_1).astype(F32)

    down, ein, sdown, sin, dense = [whole(a, b) for a, b in zip(sum_0, sum_1)]
    quarter = FF // members
    sin = jnp.concatenate(
        [
            h.reshape(members, -1, 2, quarter).transpose(1, 2, 0, 3).reshape(-1, 2 * FF) for h in sin
        ]
    )
    dense = jnp.concatenate(dense)
    at = 4 * width
    return (
        to_section(low_0, low_1),
        to_section(grad_0, grad_1),
        dense[:, at + experts : at + experts + 2].T[None],
        dense[None, :, : 3 * width],
        dense[None, :, 3 * width : at],
        dense[None, :, at : at + experts],
        sin[None],
        jnp.concatenate(sdown)[None],
        jnp.concatenate(ein)[None, None],
        jnp.concatenate(down)[None, None],
    )


def solution(mesh):
    tokens = P(None, EXP, DP, None)
    dense = P(SEC, EXP, None)
    expert = P(SEC, EXP, None, None)
    both = P(SEC, None, EXP, DP, None)
    gains = P(SEC, None, EXP)
    return jax.shard_map(
        local,
        mesh=mesh,
        in_specs=(tokens, tokens, P(), P(), tokens, P(None, EXP, DP), gains)
        + (dense,) * 5
        + (expert,) * 2,
        out_specs=(both, both, gains) + (dense,) * 5 + (expert,) * 2,
        check_vma=False,
    )
```

```python
import functools
import jax
import jax.numpy as jnp
from jax import lax
from jax.experimental import pallas as pl
from jax.experimental.pallas import tpu as pltpu
from jax.sharding import PartitionSpec as P

HEADS = 12
HEAD = 64
FF = 2048
EPS = 1e-06

SEC, DP, EXP = "section", "dp", "expert"
BF, F32, I32 = jnp.bfloat16, jnp.float32, jnp.int32
SWAP = [(0, 1), (1, 0)]


def mm(a, b, ca=1, cb=0, out=F32):
    r = lax.dot_general(a, b, (((ca,), (cb,)), ((), ())), preferred_element_type=F32)
    return r.astype(out)


def swap_cores(v):
    return lax.ppermute(v, SEC, SWAP)


def a2a(v, axis):
    return lax.all_to_all(v, axis, split_axis=0, concat_axis=0, tiled=True)


def gather(v, axis):
    return lax.all_gather(v, axis, axis=0, tiled=True)


def xor_pairs(count, k):
    return [(i, i ^ k) for i in range(count)]


def gather_blocks(v, members):
    return [v] + [lax.ppermute(v, EXP, xor_pairs(members, k)) for k in range(1, members)]


def scatter_blocks(blocks):
    count = len(blocks)
    return [blocks[0]] + [lax.ppermute(blocks[k], EXP, xor_pairs(count, k)) for k in range(1, count)]


def half_of(v, which, axis=0):
    size = v.shape[axis] // 2
    return lax.dynamic_slice_in_dim(v, which * size, size, axis)


def by_core(core, first, second):
    return jnp.where(core == 0, first, second)


def norm_apply(values, gain):
    scale = lax.rsqrt(jnp.mean(values * values, axis=-1, keepdims=True) + EPS)
    return (values * scale * gain).astype(BF), scale


def norm_backward(grad_hidden, values, scale, gain):
    normed = values * scale
    grad_gain = jnp.sum(grad_hidden * normed, axis=0)
    grad_normed = grad_hidden * gain
    grad_values = scale * (
        grad_normed - normed * jnp.mean(grad_normed * normed, axis=-1, keepdims=True)
    )
    return grad_values, grad_gain


def silu(v):
    return v * jax.nn.sigmoid(v)


def silu_parts(v):
    logistic = jax.nn.sigmoid(v)
    return v * logistic, logistic * (1.0 + v * (1.0 - logistic))


def block_mask(ends_ref, first_row, rows, cols):
    q = first_row + lax.broadcasted_iota(I32, (rows, cols), 0)
    k = lax.broadcasted_iota(I32, (rows, cols), 1)
    start = jnp.zeros((rows, cols), I32)
    for i in range(ends_ref.shape[0]):
        end = ends_ref[i]
        start = jnp.where(q >= end, end, start)
    return (k <= q) & (k >= start)


def head_slices(ref, rows, head, per, parts):
    return [ref[rows, (part * per + head) * HEAD : (part * per + head + 1) * HEAD] for part in parts]


def block_probs(q, k, mask):
    scores = lax.dot_general(q, k, (((1,), (1,)), ((), ())), preferred_element_type=F32)
    scores = jnp.where(mask, scores * (HEAD**-0.5), -1e30)
    raised = jnp.exp(scores - jnp.max(scores, axis=-1, keepdims=True))
    return raised / jnp.sum(raised, axis=-1, keepdims=True)


def attention_forward_kernel(block, per, ends_ref, qkv_ref, out_ref):
    pack = qkv_ref.shape[0]
    for i in range(pack // block):
        rows, reach = slice(i * block, (i + 1) * block), slice(0, (i + 1) * block)
        mask = block_mask(ends_ref, i * block, block, (i + 1) * block)
        for head in range(per):
            (q,) = head_slices(qkv_ref, rows, head, per, (0,))
            k, v = head_slices(qkv_ref, reach, head, per, (1, 2))
            probs = block_probs(q, k, mask).astype(BF)
            mixed = jnp.dot(probs, v, preferred_element_type=F32)
            out_ref[rows, head * HEAD : (head + 1) * HEAD] = mixed.astype(BF)


def attention_backward_kernel(block, per, ends_ref, qkv_ref, grad_ref, out_ref, dk_ref, dv_ref):
    pack = qkv_ref.shape[0]
    dk_ref[...] = jnp.zeros_like(dk_ref)
    dv_ref[...] = jnp.zeros_like(dv_ref)
    for i in range(pack // block):
        rows, reach = slice(i * block, (i + 1) * block), slice(0, (i + 1) * block)
        mask = block_mask(ends_ref, i * block, block, (i + 1) * block)
        for head in range(per):
            (q,) = head_slices(qkv_ref, rows, head, per, (0,))
            k, v = head_slices(qkv_ref, reach, head, per, (1, 2))
            grad = grad_ref[rows, head * HEAD : (head + 1) * HEAD]
            probs = block_probs(q, k, mask)
            dprobs = lax.dot_general(grad, v, (((1,), (1,)), ((), ())), preferred_element_type=F32)
            delta = jnp.sum(probs * dprobs, axis=-1, keepdims=True)
            dscores = (probs * (dprobs - delta)).astype(BF)
            dq = jnp.dot(dscores, k, preferred_element_type=F32) * (HEAD**-0.5)
            out_ref[rows, head * HEAD : (head + 1) * HEAD] = dq.astype(BF)
            over_queries = (((0,), (0,)), ((), ()))
            dk_ref[head, reach, :] += lax.dot_general(
                dscores, q, over_queries, preferred_element_type=F32
            )
            dv_ref[head, reach, :] += lax.dot_general(
                probs.astype(BF), grad, over_queries, preferred_element_type=F32
            )
    for head in range(per):
        at = (per + head) * HEAD
        out_ref[:, at : at + HEAD] = (dk_ref[head] * (HEAD**-0.5)).astype(BF)
        at = (2 * per + head) * HEAD
        out_ref[:, at : at + HEAD] = dv_ref[head].astype(BF)


def vmem():
    return pl.BlockSpec(memory_space=pltpu.VMEM)


def attention_forward(ends, qkv, block):
    pack, columns = qkv.shape
    per = columns // (3 * HEAD)
    return pl.pallas_call(
        functools.partial(attention_forward_kernel, block, per),
        out_shape=jax.ShapeDtypeStruct((pack, per * HEAD), BF),
        in_specs=[pl.BlockSpec(memory_space=pltpu.SMEM), vmem()],
        out_specs=vmem(),
        compiler_params=pltpu.CompilerParams(vmem_limit_bytes=32 << 20),
        cost_estimate=pl.CostEstimate(
            flops=4 * per * pack * pack * HEAD, bytes_accessed=8 * pack * columns // 3, transcendentals=per * pack * pack
        ),
    )(ends, qkv)


def attention_backward(ends, qkv, grad, block):
    pack, columns = qkv.shape
    per = columns // (3 * HEAD)
    return pl.pallas_call(
        functools.partial(attention_backward_kernel, block, per),
        out_shape=jax.ShapeDtypeStruct((pack, columns), BF),
        in_specs=[pl.BlockSpec(memory_space=pltpu.SMEM), vmem(), vmem()],
        out_specs=vmem(),
        scratch_shapes=[pltpu.VMEM((per, pack, HEAD), F32)] * 2,
        compiler_params=pltpu.CompilerParams(vmem_limit_bytes=32 << 20),
        cost_estimate=pl.CostEstimate(
            flops=10 * per * pack * pack * HEAD, bytes_accessed=16 * pack * columns // 3, transcendentals=per * pack * pack
        ),
    )(ends, qkv, grad)


SPOT = 64
TAIL = 16
TILE = 512
WINDOW_STEP = (1, 2)
TAIL_STEP = (1, 2)
CHUNKS = (1, 2, 1, 1, 1)


def nt(a, b):
    return lax.dot_general(a, b, (((1,), (1,)), ((), ())), preferred_element_type=F32)


def nn(a, b):
    return jnp.dot(a, b, preferred_element_type=F32)


def slot_rows(slot_ref, k, first, count):
    row = slot_ref[k : k + 1, :]
    place = first + lax.broadcasted_iota(I32, (count, row.shape[1]), 0)
    return (place == row).astype(F32).astype(BF)


def slot_columns(info, capacity):
    column = info[:, SPOT : SPOT + 1]
    place = lax.broadcasted_iota(I32, (info.shape[0], capacity), 1).astype(F32)
    return (place == column).astype(F32).astype(BF)


def dispatch(slot_ref, block_refs, first, count):
    total = None
    for k, ref in enumerate(block_refs):
        part = nn(slot_rows(slot_ref, k, first, count), ref[...])
        total = part if total is None else total + part
    return total.astype(BF)


def from_either(which_ref, sources, body):
    @pl.when(which_ref[1] == 1)
    def _():
        body(*sources[0])

    @pl.when(which_ref[1] == 0)
    def _():
        body(*sources[1])


def moe_forward_kernel(members, experts, *refs):
    which_ref, slot_ref, info_ref, router_ref = refs[:4]
    h_refs, refs = refs[4 : 4 + members], refs[4 + members :]
    sources, (wsi_ref, wsd_ref), refs = (refs[:3], refs[3:6]), refs[6:8], refs[3:]
    rows_ref, g_ref, u_ref, a_ref, meta_ref, ret_ref, sg_ref, su_ref, sa_ref = refs[5:14]
    part_refs, (acc_ref, y_ref) = refs[14 : 14 + members], refs[14 + members :]
    step, last = pl.program_id(0), pl.num_programs(0) - 1
    capacity, tokens = rows_ref.shape[0], h_refs[0].shape[0]
    tiles = [slice(r, r + tokens) for r in range(0, capacity, tokens)]

    @pl.when(step == 0)
    def _():
        for r in tiles:
            rows_ref[r, :] = dispatch(slot_ref, h_refs, r.start, tokens)
            acc_ref[r, :] = jnp.zeros((tokens, acc_ref.shape[1]), F32)

    def units(wg_ref, wu_ref, wd_ref):
        for r in tiles:
            x = rows_ref[r, :]
            gate, up = nn(x, wg_ref[...]), nn(x, wu_ref[...])
            act = (gate * jax.nn.sigmoid(gate) * up).astype(BF)
            g_ref[r, :], u_ref[r, :], a_ref[r, :] = gate.astype(BF), up.astype(BF), act
            acc_ref[r, :] += nn(act, wd_ref[...])

    from_either(which_ref, sources, units)

    @pl.when(step == last)
    def _():
        for r in tiles:
            y_ref[r, :] = acc_ref[r, :].astype(BF)
        quarter = wsd_ref.shape[0]
        for k in range(members):
            t = slice(k * tokens, (k + 1) * tokens)
            h, info = h_refs[k][...], info_ref[t, :]
            lane = lax.broadcasted_iota(I32, info.shape, 1)
            logits = jnp.where(lane < experts, nn(h, router_ref[...]), -1e30)
            raised = jnp.exp(logits - jnp.max(logits, axis=-1, keepdims=True))
            probs = raised / jnp.sum(raised, axis=-1, keepdims=True)
            chosen = jnp.where(lane < experts, info, 0.0)
            picked = jnp.sum(probs * chosen, axis=-1, keepdims=True)
            here = jnp.sum(jnp.where(lane == which_ref[0], probs, 0.0), axis=-1, keepdims=True)
            weight = here / picked
            meta_ref[t, :] = jnp.where(lane == SPOT, weight, probs)
            gate, up = nn(h, wsi_ref[:, :quarter]), nn(h, wsi_ref[:, quarter:])
            act = (gate * jax.nn.sigmoid(gate) * up).astype(BF)
            sg_ref[t, :], su_ref[t, :], sa_ref[t, :] = gate.astype(BF), up.astype(BF), act
            back = nn(slot_columns(info, capacity), y_ref[...])
            ret_ref[t, :] = back.astype(BF)
            part_refs[k][...] = (weight * back + nn(act, wsd_ref[...])).astype(BF)


def act_grads(gate_low, up_low, grad_act):
    gate, up = gate_low.astype(F32), up_low.astype(F32)
    value, slope = silu_parts(gate)
    return (grad_act * up * slope).astype(BF), (grad_act * value).astype(BF)


def moe_backward_kernel(members, *refs):
    which_ref, slot_ref, info_ref, meta_ref = refs[:4]
    grad_refs, refs = refs[4 : 4 + members], refs[4 + members :]
    ret_ref, sources, refs = refs[0], (refs[1:4], refs[4:7]), refs[7:]
    g_ref, u_ref, sg_ref, su_ref, wsi_ref, wsd_ref = refs[:6]
    dy_ref, dg_ref, du_ref, dsg_ref, dsu_ref = refs[6:11]
    part_refs, (gated_ref, acc_ref) = refs[11 : 11 + members], refs[11 + members :]
    step, last = pl.program_id(0), pl.num_programs(0) - 1
    capacity, width = dy_ref.shape
    tokens = grad_refs[0].shape[0]
    tiles = [slice(r, r + tokens) for r in range(0, capacity, tokens)]

    @pl.when(step == 0)
    def _():
        for k in range(members):
            t = slice(k * tokens, (k + 1) * tokens)
            grad = grad_refs[k][...].astype(F32)
            weight = meta_ref[t, SPOT : SPOT + 1]
            gated_ref[k, :, :] = (weight * grad).astype(BF)
            product = grad * ret_ref[t, :].astype(F32)
            high = product.astype(BF)
            low = (product - high.astype(F32)).astype(BF)
            ones = jnp.ones((TAIL, width), BF)
            total = nt(ones, high) + nt(ones, low)
            high = total.astype(BF).astype(F32)
            row = lax.broadcasted_iota(I32, total.shape, 0)
            tail = jnp.where(row == 0, high, jnp.where(row == 1, total - high, 0.0))
            part_refs[k][tokens : tokens + TAIL, :] = jnp.zeros((TAIL, width), BF)
            part_refs[k][tokens : tokens + TAIL, :tokens] = tail.astype(BF)
        for r in tiles:
            dy_ref[r, :] = dispatch(slot_ref, [gated_ref.at[k] for k in range(members)], r.start, tokens)
            acc_ref[r, :] = jnp.zeros((tokens, width), F32)

    def units(wg_ref, wu_ref, wd_ref):
        for r in tiles:
            dg, du = act_grads(g_ref[r, :], u_ref[r, :], nt(dy_ref[r, :], wd_ref[...]))
            dg_ref[r, :], du_ref[r, :] = dg, du
            acc_ref[r, :] += nt(dg, wg_ref[...]) + nt(du, wu_ref[...])

    from_either(which_ref, sources, units)

    @pl.when(step == last)
    def _():
        rows = acc_ref[...].astype(BF)
        quarter = wsd_ref.shape[0]
        for k in range(members):
            t = slice(k * tokens, (k + 1) * tokens)
            dsg, dsu = act_grads(sg_ref[t, :], su_ref[t, :], nt(grad_refs[k][...], wsd_ref[...]))
            dsg_ref[t, :], dsu_ref[t, :] = dsg, dsu
            back = nt(dsg, wsi_ref[:, :quarter]) + nt(dsu, wsi_ref[:, quarter:])
            back = back + nn(slot_columns(info_ref[t, :], capacity), rows)
            part_refs[k][:tokens, :] = back.astype(BF)


def whole_block(*shape):
    return pl.BlockSpec(shape, lambda i, which: (0,) * len(shape), pipeline_mode=pl.Buffered(1))


def expert_specs(width):
    steps = FF // TILE

    def tiles(own):
        def at(i, which):
            return i * (which[1] if own else 1 - which[1])

        return [
            pl.BlockSpec((width, TILE), lambda i, which: (0, at(i, which))),
            pl.BlockSpec((width, TILE), lambda i, which: (0, steps + at(i, which))),
            pl.BlockSpec((TILE, width), lambda i, which: (at(i, which), 0)),
        ]

    return tiles(True) + tiles(False)


def expert_args(experts):
    return [w for w_in, w_down in experts for w in (w_in, w_in, w_down)]


def moe_call(kernel, shapes, in_specs, out_tiled, scratch, args, work):
    whole = [whole_block(*shape) for shape, _ in shapes]
    tiled = pl.BlockSpec((shapes[0][0][0], TILE), lambda i, which: (0, i))
    return pl.pallas_call(
        kernel,
        out_shape=[jax.ShapeDtypeStruct(*shape) for shape in shapes],
        grid_spec=pltpu.PrefetchScalarGridSpec(
            num_scalar_prefetch=1,
            grid=(FF // TILE,),
            in_specs=in_specs,
            out_specs=whole[:1] + [tiled] * out_tiled + whole[1 + out_tiled :],
            scratch_shapes=scratch,
        ),
        compiler_params=pltpu.CompilerParams(vmem_limit_bytes=56 << 20),
        cost_estimate=pl.CostEstimate(flops=work, bytes_accessed=30 << 20, transcendentals=1 << 20),
    )(*args)


def moe_work(width, capacity, everyone, quarter):
    return 2 * width * (capacity * (3 * FF + 2 * everyone) + 3 * everyone * quarter)


def moe_forward(which, slot, info, w_small, blocks, experts, w_sin, w_sdown, capacity, count):
    members, (tokens, width), quarter = len(blocks), blocks[0].shape, w_sdown.shape[0]
    everyone = members * tokens
    shapes = [((capacity, width), BF)] + [((capacity, FF), BF)] * 3
    shapes += [((everyone, 128), F32), ((everyone, width), BF)] + [((everyone, quarter), BF)] * 3
    shapes += [((tokens, width), BF)] * members
    in_specs = [whole_block(members, tokens), whole_block(everyone, 128), whole_block(width, 128)]
    in_specs += [whole_block(tokens, width)] * members + expert_specs(width)
    in_specs += [whole_block(width, 2 * quarter), whole_block(quarter, width)]
    return moe_call(
        functools.partial(moe_forward_kernel, members, count),
        shapes,
        in_specs,
        3,
        [pltpu.VMEM((capacity, width), F32), pltpu.VMEM((capacity, width), BF)],
        (which, slot, info, w_small, *blocks, *expert_args(experts), w_sin, w_sdown),
        moe_work(width, capacity, everyone, quarter),
    )


def moe_backward(which, slot, info, meta, blocks, ret, experts, gate, up, sg, su, w_sin, w_sdown):
    members, (tokens, width), quarter = len(blocks), blocks[0].shape, w_sdown.shape[0]
    everyone, capacity = members * tokens, gate.shape[0]
    shapes = [((capacity, width), BF)] + [((capacity, FF), BF)] * 2
    shapes += [((everyone, quarter), BF)] * 2 + [((tokens + TAIL, width), BF)] * members
    in_specs = [whole_block(members, tokens), whole_block(everyone, 128), whole_block(everyone, 128)]
    in_specs += [whole_block(tokens, width)] * members + [whole_block(everyone, width)] + expert_specs(width)
    in_specs += [pl.BlockSpec((capacity, TILE), lambda i, which: (0, i))] * 2
    in_specs += [whole_block(everyone, quarter)] * 2
    in_specs += [whole_block(width, 2 * quarter), whole_block(quarter, width)]
    return moe_call(
        functools.partial(moe_backward_kernel, members),
        shapes,
        in_specs,
        2,
        [pltpu.VMEM((members, tokens, width), BF), pltpu.VMEM((capacity, width), F32)],
        (which, slot, info, meta, *blocks, ret, *expert_args(experts), gate, up, sg, su, w_sin, w_sdown),
        moe_work(width, capacity, everyone, quarter),
    )


def after(values, *others):
    return lax.optimization_barrier((values, others))[0]


class Weights:
    def __init__(self, core, members, gains, w_qkv, w_out, w_router, *rest):
        self.core, self.members, self.width = core, members, w_out.shape[1]
        self.experts = w_router.shape[1]
        rows, extra = w_qkv.shape[0], self.experts + 2
        small = jnp.concatenate([w_router, gains.T, jnp.zeros((rows, 128 - extra), BF)], axis=1)
        self.first_shares = self.shares(jnp.concatenate([w_qkv, small], axis=1))
        self.out_shares = self.shares(w_out)
        self.w_sin, self.w_sdown, self.w_ein, self.w_edown = rest

    def both(self, mine):
        other = swap_cores(mine)
        return by_core(self.core, mine, other), by_core(self.core, other, mine)

    def shares(self, shard):
        mine, theirs = half_of(shard, self.core), half_of(shard, 1 - self.core)
        other = swap_cores(theirs)
        return by_core(self.core, mine, other), by_core(self.core, other, mine)

    def both_halves(self, full):
        blocks, rows, columns = full.shape
        other = swap_cores(full)
        halves = [by_core(self.core, full, other), by_core(self.core, other, full)]
        return jnp.stack(halves, axis=1).reshape(blocks * 2 * rows, columns)

    def permuted(self, part):
        me, blocks = lax.axis_index(EXP), jnp.stack(gather_blocks(part, self.members))
        return jnp.concatenate(
            [lax.dynamic_slice_in_dim(blocks, me ^ j, 1, 0) for j in range(self.members)]
        )

    def split_first(self, first):
        at = 3 * self.width
        small = first[:, at : at + 128]
        return first[:, :at], small, small[:, self.experts : self.experts + 2].T.astype(F32)

    def shared_in(self, w_sin):
        me, quarter = lax.axis_index(EXP), FF // self.members
        blocks = []
        for k in range(self.members):
            at = (me ^ k) * quarter
            parts = [lax.dynamic_slice_in_dim(w_sin, start + at, quarter, 1) for start in (0, FF)]
            blocks.append(jnp.concatenate(parts, axis=1))
        blocks = jnp.stack(scatter_blocks(blocks))
        return jnp.concatenate([lax.dynamic_index_in_dim(blocks, me ^ j, 0, False) for j in range(self.members)])


def add_low(a, b):
    return (a.astype(F32) + b.astype(F32)).astype(BF)


class LineSums:
    def __init__(self):
        lane = lax.axis_index(DP)
        self.middle = (lane == 1) | (lane == 2)
        self.now, self.waiting, self.flights, self.done = 0, [], [], {}

    def add(self, section, name, chunks):
        self.waiting += [((section, name, i), chunk) for i, chunk in enumerate(chunks)]

    def busy(self):
        return self.waiting or self.flights

    def step(self, main, count=WINDOW_STEP[0], steps=WINDOW_STEP[1]):
        self.now += 1
        landed = [flight for flight in self.flights if flight[0] <= self.now]
        self.flights = [flight for flight in self.flights if flight[0] > self.now]
        fresh, self.waiting = self.waiting[:count], self.waiting[count:]
        tied = (main, [flight[3:] for flight in landed], [item[1] for item in fresh])
        main, states, chunks = lax.optimization_barrier(tied)

        def launch(stage, key, value, axis, pairs, wait):
            got = lax.ppermute(value, axis, pairs)
            self.flights.append((self.now + wait, stage, key, value, got))

        for (_, stage, key, *_), (value, got) in zip(landed, states):
            if stage == 0:
                launch(1, key, add_low(value, got), DP, [(1, 2), (2, 1)], steps)
            elif stage == 1:
                launch(2, key, add_low(value, got), DP, [(1, 0), (2, 3)], steps)
            elif stage == 2:
                pair = (1, 0) if key[0] == 0 else (0, 1)
                launch(3, key, jnp.where(self.middle, value, got), SEC, [pair], 1)
            else:
                self.done[key] = (value, got)
        for (key, _), chunk in zip(fresh, chunks):
            launch(0, key, chunk, DP, [(0, 1), (3, 2)], steps)
        return main

    def result(self, section, name):
        keys = sorted(key for key in self.done if key[:2] == (section, name))
        return [self.done[key] for key in keys]


def cut(v, count):
    rows = v.shape[0] // count
    return [v[i * rows : (i + 1) * rows] for i in range(count)]


def to_heads(v, lanes, parts):
    tokens, columns = v.shape
    per = columns // (parts * lanes)
    split = v.reshape(tokens, parts, lanes, per).transpose(2, 0, 1, 3).reshape(lanes, tokens, parts * per)
    return a2a(split, DP).reshape(lanes * tokens, parts * per)


def to_tokens(v, lanes, parts):
    pack, columns = v.shape
    tokens, per = pack // lanes, columns // parts
    got = a2a(v.reshape(lanes, tokens, columns), DP).reshape(lanes, tokens, parts, per)
    return got.transpose(1, 2, 0, 3).reshape(tokens, lanes * columns)


def add_blocks(first, blocks):
    return functools.reduce(jnp.add, [block.astype(F32) for block in blocks], first)


def layer_mlp(middle, context, weights, beside=None):
    gain, w_small, w_sin, w_sdown, experts, which = weights
    me, slot, info, capacity, count = context
    members = slot.shape[0]
    hidden, scale = norm_apply(middle, gain)
    blocks = gather_blocks(hidden, members)
    out = moe_forward(which, slot, info, w_small, blocks, experts, w_sin, w_sdown, capacity, count)
    if beside is not None:
        out = beside(out)
    parts = scatter_blocks(out[9:])
    return add_blocks(middle, parts), (scale, hidden, blocks, *out[:9])


def mlp_backward(grad_blocks, middle, saved, context, weights, sums, ready):
    gain, w_small, w_sin, w_sdown, expert_weights, which = weights
    me, slot, info, capacity, experts = context
    scale, hidden, blocks, rows, gate, up, act, meta, ret, sg, su, sact = saved
    members, (tokens, width) = len(blocks), middle.shape
    out = moe_backward(
        which, slot, info, meta, grad_blocks, ret, expert_weights, gate, up, sg, su, w_sin, w_sdown
    )
    out = sums.step(out)
    dy, dg, du, dsg, dsu = out[:5]
    parts = scatter_blocks(out[5:])
    ready((rows, act, dy, dg, du), (blocks, sact, grad_blocks, dsg, dsu))
    parts = sums.step(parts)
    dh2 = add_blocks(jnp.zeros(middle.shape, F32), [part[:tokens] for part in parts])
    tails = [part[tokens : tokens + 2, :tokens].astype(F32) for part in parts]
    column = jnp.arange(experts, dtype=I32)[None, :]
    dgates = sum(
        jnp.where(column == (me ^ k), (tail[0] + tail[1])[:, None], 0.0) for k, tail in enumerate(tails)
    )
    router, chosen = meta[:tokens, :experts], info[:tokens, :experts]
    picked = jnp.sum(router * chosen, axis=-1, keepdims=True)
    inner = jnp.sum(dgates * router * chosen, axis=-1, keepdims=True) / picked
    dprob = chosen * (dgates - inner) / picked
    dlogits = (router * (dprob - jnp.sum(router * dprob, axis=-1, keepdims=True))).astype(BF)
    dh2 = dh2 + mm(dlogits, w_small[:, :experts], 1, 1)
    dmiddle_norm, dgain = norm_backward(dh2, middle, scale, gain)
    dmiddle = grad_blocks[0].astype(F32) + dmiddle_norm
    return dmiddle, dgain, dlogits


def halves(rows_of, grads, core):
    send = mm(half_of(rows_of, 1 - core, 1), grads, 0, 0, out=BF)
    keep = mm(half_of(rows_of, core, 1), grads, 0, 0)
    return (keep + swap_cores(send).astype(F32)).astype(BF)


def halves_by_member(rows_of, grads, core, members):
    split = rows_of.reshape(rows_of.shape[0], members, 2, -1)

    def side(which):
        return lax.dynamic_index_in_dim(split, which, 2, False).reshape(rows_of.shape[0], -1)

    send = mm(side(1 - core), grads, 0, 0, out=BF)
    keep = mm(side(core), grads, 0, 0)
    return (keep + swap_cores(send).astype(F32)).astype(BF).reshape(members, -1, grads.shape[1])


def expert_grads(terms, core):
    rows, act, dy, dg, du = terms
    g_in = jnp.concatenate([halves(rows, dg, core), halves(rows, du, core)], axis=1)
    return halves(act, dy, core), g_in


def shared_grads(terms, core):
    blocks, sact, grad_blocks, dsg, dsu = terms
    members = len(blocks)
    hidden_all, grad_all = jnp.concatenate(blocks), jnp.concatenate(grad_blocks)
    g_in = halves_by_member(hidden_all, jnp.concatenate([dsg, dsu], axis=1), core, members)
    return halves(sact, grad_all, core), a2a(g_in, EXP)


def dense_grads(terms, core, members):
    hidden_one, dqkv, mixed, dattn, hidden_two, dlogits, dgains = terms
    width, experts = hidden_one.shape[1], dlogits.shape[1]
    small = jnp.concatenate(
        [mm(hidden_two, dlogits, 0, 0), jnp.stack(dgains, axis=1), jnp.zeros((width, 126 - experts), F32)],
        axis=1,
    )
    split = small.reshape(members, 2, -1, 128)
    send = lax.dynamic_index_in_dim(split, 1 - core, 1, False).astype(BF)
    keep = lax.dynamic_index_in_dim(split, core, 1, False)
    small = (keep + swap_cores(send).astype(F32)).astype(BF)
    g_out = halves_by_member(mixed, dattn, core, members)
    g_qkv = halves_by_member(hidden_one, dqkv, core, members)
    parts = a2a(jnp.concatenate([g_qkv, g_out, small], axis=2), EXP)
    return jnp.sum(parts.astype(F32), axis=0).astype(BF)


def local(
    inputs, cotangent, lengths, deal, routes, order, gains, w_qkv, w_out, w_router, w_shared_in, w_shared_down,
    w_expert_in, w_expert_down,
):
    core, me = lax.axis_index(SEC), lax.axis_index(EXP)
    members, lanes = lax.axis_size(EXP), lax.axis_size(DP)
    batches, _, tokens, width = inputs.shape
    experts = w_router.shape[2]
    assert batches == lax.axis_size(SEC) == 2 and w_expert_in.shape[1] == 1 and experts == members
    w = Weights(
        core, members, gains[0], w_qkv[0], w_out[0], w_router[0], w_shared_in[0], w_shared_down[0],
        w_expert_in[0, 0], w_expert_down[0, 0],
    )
    first_low = lax.dynamic_index_in_dim(inputs[:, 0], core, 0, False)
    grad_low = lax.dynamic_index_in_dim(cotangent[:, 0], core, 0, False)
    row = lax.dynamic_index_in_dim(deal, core * members + me, 0, False)
    ends = jnp.cumsum(lax.dynamic_index_in_dim(lengths, row, 0, False))[:-1].astype(I32)
    qkv_0, w_small_0, gains_0 = w.split_first(w.both_halves(w.permuted(w.first_shares[0])))
    current_0 = first_low.astype(F32)
    hidden_0, scale_0 = norm_apply(current_0, gains_0[0])
    projected = mm(hidden_0, qkv_0, out=BF)
    pairs = lax.dynamic_index_in_dim(routes[:, 0], core, 0, False).reshape(-1)
    places = lax.dynamic_index_in_dim(order[:, 0], core, 0, False)
    same = pairs[:, None] == pairs[None, :]
    rank = jnp.sum((same & (places[None, :] < places[:, None])).astype(I32), axis=1)
    code = jnp.stack(gather_blocks(after(pairs * (2 * tokens) + rank, projected), members))
    owner = me ^ jnp.arange(members, dtype=I32)
    pairs_all, rank_all = code // (2 * tokens), code % (2 * tokens)
    onehot = (pairs_all[:, :, None] == jnp.arange(experts, dtype=I32)).astype(I32)
    counts = jnp.sum(onehot, axis=1)
    lower = (owner[None, :] < owner[:, None]).astype(I32)
    before = jnp.sum(lower[:, :, None] * counts[None], axis=1)
    place = jnp.sum(onehot * before[:, None, :], axis=2) + rank_all
    capacity = 2 * tokens * members // experts
    slot = jnp.where((pairs_all == me) & (place < capacity), place, -1)
    slot = jnp.max(slot.reshape(members, tokens, 2), axis=2)
    column = jnp.arange(128, dtype=I32)[None, :]
    named = pairs_all.reshape(members * tokens, 2)
    chosen = (named[:, :1] == column) | (named[:, 1:] == column)
    info = jnp.where(column == SPOT, slot.reshape(-1, 1).astype(F32), chosen.astype(F32))

    w_out_0 = w.both_halves(w.permuted(after(w.out_shares[0], projected)))
    shared_in = w.shared_in(after(w.w_sin, projected))
    shared = (shared_in, w.w_sdown)
    shared = (shared, (swap_cores(shared_in), swap_cores(w.w_sdown)))
    expert_weights = ((w.w_ein, w.w_edown), (swap_cores(w.w_ein), swap_cores(w.w_edown)))
    which = [jnp.stack([me, (core == s).astype(I32)]) for s in range(2)]
    heads_0 = to_heads(projected, lanes, 3)
    heads_0, slot, info, w_out_0 = lax.optimization_barrier((heads_0, slot, info, w_out_0))
    context = (me, slot, info, capacity, experts)
    later = jnp.concatenate([w.first_shares[1], w.out_shares[1]], axis=1)
    mixed_0, shared = lax.optimization_barrier((attention_forward(ends, heads_0, tokens), shared))
    mixed_0 = to_tokens(mixed_0, lanes, 1)
    shared_first = [by_core(core, mine, other) for mine, other in zip(*shared)]
    mixed_0, shared_first = lax.optimization_barrier((mixed_0, shared_first))
    shared_second = [by_core(core, other, mine) for mine, other in zip(*shared)]
    middle_0 = current_0 + mm(mixed_0, w_out_0)
    gathered = []

    def land(out):
        out, full = lax.optimization_barrier((out, lax.all_gather(after(later, middle_0), EXP)))
        gathered.append(full)
        return out

    mlp_0 = (gains_0[1], w_small_0, *shared_first, expert_weights, which[0])
    out_0, saved_0 = layer_mlp(middle_0, context, mlp_0, land)
    dense_1 = w.both_halves(gathered[0])
    low_0, dense_1, shared_second = lax.optimization_barrier((out_0.astype(BF), dense_1, shared_second))
    qkv_1, w_small_1, gains_1 = w.split_first(dense_1)
    w_out_1 = dense_1[:, 3 * width + 128 :]
    current_1 = low_0.astype(F32)
    hidden_1, scale_1 = norm_apply(current_1, gains_1[0])
    projected = mm(hidden_1, qkv_1, out=BF)
    grad_blocks = gather_blocks(after(grad_low, projected), members)
    heads_1 = to_heads(projected, lanes, 3)
    heads_1, grad_blocks = lax.optimization_barrier((heads_1, grad_blocks))
    mixed_1 = to_tokens(attention_forward(ends, heads_1, tokens), lanes, 1)
    middle_1 = current_1 + mm(mixed_1, w_out_1)
    mlp_1 = (gains_1[1], w_small_1, *shared_second, expert_weights, which[1])
    out_1, saved_1 = layer_mlp(middle_1, context, mlp_1)
    low_1 = out_1.astype(BF)

    sums = LineSums()

    def backward(section, grad_blocks, current, hidden, scale, heads, mixed, middle, saved, gain, w_qkv_s, w_out_s, mlp):
        shared = []

        def ready(terms, shared_terms):
            down, ein = expert_grads(terms, core)
            sums.add(section, 0, cut(down, CHUNKS[0]))
            sums.add(section, 1, cut(ein, CHUNKS[1]))
            shared.append(shared_terms)

        dmiddle, dgain_two, dlogits = mlp_backward(grad_blocks, middle, saved, context, mlp, sums, ready)
        dattn = dmiddle.astype(BF)
        dheads = to_heads(mm(dattn, w_out_s, 1, 1, out=BF), lanes, 1)
        g_sdown, g_sin = shared_grads(shared[0], core)
        sums.add(section, 2, [g_sdown])
        sums.add(section, 3, [g_sin.reshape(-1, g_sin.shape[2])])
        dheads = sums.step(dheads)
        dheads = sums.step(attention_backward(ends, heads, dheads, tokens))
        dqkv = sums.step(to_tokens(dheads, lanes, 3))
        dinput, dgain_one = norm_backward(mm(dqkv, w_qkv_s, 1, 1), current, scale, gain)
        dense = (hidden, dqkv, mixed, dattn, saved[1], dlogits, (dgain_one, dgain_two))
        sums.add(section, 4, [dense_grads(dense, core, members)])
        return dmiddle + dinput

    grad_1 = backward(
        1, grad_blocks, current_1, hidden_1, scale_1, heads_1, mixed_1, middle_1, saved_1, gains_1[0], qkv_1,
        w_out_1, mlp_1,
    )
    grad_blocks = sums.step(gather_blocks(grad_1.astype(BF), members))
    grad_0 = backward(
        0, grad_blocks, current_0, hidden_0, scale_0, heads_0, mixed_0, middle_0, saved_0, gains_0[0], qkv_0,
        w_out_0, mlp_0,
    )
    quarter = FF // members

    def by_columns(half):
        blocks = half.reshape(members, -1, 2 * quarter)
        return jnp.concatenate(
            [blocks[j][:, at : at + quarter] for at in (0, quarter) for j in range(members)], axis=1
        )

    def whole(name):
        own_0, got_0 = zip(*sums.result(0, name))
        own_1, got_1 = zip(*sums.result(1, name))
        pairs = zip(own_0 + got_0, got_1 + own_1)
        parts = [by_core(core, a, b) for a, b in pairs]
        return jnp.concatenate([by_columns(v) if name == 3 else v for v in parts]).astype(F32)

    def complete(name):
        return all(len(sums.result(section, name)) == CHUNKS[name] for section in range(2))

    results = {}
    while sums.busy():
        results = sums.step(results, *TAIL_STEP)
        results.update({name: whole(name) for name in range(5) if name not in results and complete(name)})

    def to_section(of_0, of_1):
        mine = by_core(core, of_0, of_1)
        other = swap_cores(by_core(core, of_1, of_0))
        both = jnp.stack([by_core(core, mine, other), by_core(core, other, mine)])
        return both[None, :, None]

    down, ein, sdown, sin, dense = [results[name] for name in range(5)]
    at = 4 * width
    return (
        to_section(low_0, low_1),
        to_section(grad_0, grad_1),
        dense[:, at + experts : at + experts + 2].T[None],
        dense[None, :, : 3 * width],
        dense[None, :, 3 * width : at],
        dense[None, :, at : at + experts],
        sin[None],
        sdown[None],
        ein[None, None],
        down[None, None],
    )


def solution(mesh):
    tokens = P(None, EXP, DP, None)
    dense = P(SEC, EXP, None)
    expert = P(SEC, EXP, None, None)
    both = P(SEC, None, EXP, DP, None)
    gains = P(SEC, None, EXP)
    return jax.shard_map(
        local,
        mesh=mesh,
        in_specs=(tokens, tokens, P(), P(), tokens, P(None, EXP, DP), gains)
        + (dense,) * 5
        + (expert,) * 2,
        out_specs=(both, both, gains) + (dense,) * 5 + (expert,) * 2,
        check_vma=False,
    )
```

```python
import functools
import jax
import jax.numpy as jnp
from jax import lax
from jax.experimental import pallas as pl
from jax.experimental.pallas import tpu as pltpu
from jax.sharding import PartitionSpec as P

HEADS = 12
HEAD = 64
FF = 2048
EPS = 1e-06

SEC, DP, EXP = "section", "dp", "expert"
BF, F32, I32 = jnp.bfloat16, jnp.float32, jnp.int32
SWAP = [(0, 1), (1, 0)]


def mm(a, b, ca=1, cb=0, out=F32):
    r = lax.dot_general(a, b, (((ca,), (cb,)), ((), ())), preferred_element_type=F32)
    return r.astype(out)


def swap_cores(v):
    return lax.ppermute(v, SEC, SWAP)


def a2a(v, axis):
    return lax.all_to_all(v, axis, split_axis=0, concat_axis=0, tiled=True)


def gather(v, axis):
    return lax.all_gather(v, axis, axis=0, tiled=True)


def xor_pairs(count, k):
    return [(i, i ^ k) for i in range(count)]


def gather_blocks(v, members):
    return [v] + [lax.ppermute(v, EXP, xor_pairs(members, k)) for k in range(1, members)]


def scatter_blocks(blocks):
    count = len(blocks)
    return [blocks[0]] + [lax.ppermute(blocks[k], EXP, xor_pairs(count, k)) for k in range(1, count)]


def half_of(v, which, axis=0):
    size = v.shape[axis] // 2
    return lax.dynamic_slice_in_dim(v, which * size, size, axis)


def by_core(core, first, second):
    return jnp.where(core == 0, first, second)


def norm_apply(values, gain):
    scale = lax.rsqrt(jnp.mean(values * values, axis=-1, keepdims=True) + EPS)
    return (values * scale * gain).astype(BF), scale


def norm_backward(grad_hidden, values, scale, gain):
    normed = values * scale
    grad_gain = jnp.sum(grad_hidden * normed, axis=0)
    grad_normed = grad_hidden * gain
    grad_values = scale * (
        grad_normed - normed * jnp.mean(grad_normed * normed, axis=-1, keepdims=True)
    )
    return grad_values, grad_gain


def silu(v):
    return v * jax.nn.sigmoid(v)


def silu_parts(v):
    logistic = jax.nn.sigmoid(v)
    return v * logistic, logistic * (1.0 + v * (1.0 - logistic))


def block_mask(ends_ref, first_row, rows, cols):
    q = first_row + lax.broadcasted_iota(I32, (rows, cols), 0)
    k = lax.broadcasted_iota(I32, (rows, cols), 1)
    start = jnp.zeros((rows, cols), I32)
    for i in range(ends_ref.shape[0]):
        end = ends_ref[i]
        start = jnp.where(q >= end, end, start)
    return (k <= q) & (k >= start)


def head_slices(ref, rows, head, per, parts):
    return [ref[rows, (part * per + head) * HEAD : (part * per + head + 1) * HEAD] for part in parts]


def block_probs(q, k, mask):
    scores = lax.dot_general(q, k, (((1,), (1,)), ((), ())), preferred_element_type=F32)
    scores = jnp.where(mask, scores * (HEAD**-0.5), -1e30)
    raised = jnp.exp(scores - jnp.max(scores, axis=-1, keepdims=True))
    return raised / jnp.sum(raised, axis=-1, keepdims=True)


def attention_forward_kernel(block, per, ends_ref, qkv_ref, out_ref):
    pack = qkv_ref.shape[0]
    for i in range(pack // block):
        rows, reach = slice(i * block, (i + 1) * block), slice(0, (i + 1) * block)
        mask = block_mask(ends_ref, i * block, block, (i + 1) * block)
        for head in range(per):
            (q,) = head_slices(qkv_ref, rows, head, per, (0,))
            k, v = head_slices(qkv_ref, reach, head, per, (1, 2))
            probs = block_probs(q, k, mask).astype(BF)
            mixed = jnp.dot(probs, v, preferred_element_type=F32)
            out_ref[rows, head * HEAD : (head + 1) * HEAD] = mixed.astype(BF)


def attention_backward_kernel(block, per, ends_ref, qkv_ref, grad_ref, out_ref, dk_ref, dv_ref):
    pack = qkv_ref.shape[0]
    dk_ref[...] = jnp.zeros_like(dk_ref)
    dv_ref[...] = jnp.zeros_like(dv_ref)
    for i in range(pack // block):
        rows, reach = slice(i * block, (i + 1) * block), slice(0, (i + 1) * block)
        mask = block_mask(ends_ref, i * block, block, (i + 1) * block)
        for head in range(per):
            (q,) = head_slices(qkv_ref, rows, head, per, (0,))
            k, v = head_slices(qkv_ref, reach, head, per, (1, 2))
            grad = grad_ref[rows, head * HEAD : (head + 1) * HEAD]
            probs = block_probs(q, k, mask)
            dprobs = lax.dot_general(grad, v, (((1,), (1,)), ((), ())), preferred_element_type=F32)
            delta = jnp.sum(probs * dprobs, axis=-1, keepdims=True)
            dscores = (probs * (dprobs - delta)).astype(BF)
            dq = jnp.dot(dscores, k, preferred_element_type=F32) * (HEAD**-0.5)
            out_ref[rows, head * HEAD : (head + 1) * HEAD] = dq.astype(BF)
            over_queries = (((0,), (0,)), ((), ()))
            dk_ref[head, reach, :] += lax.dot_general(
                dscores, q, over_queries, preferred_element_type=F32
            )
            dv_ref[head, reach, :] += lax.dot_general(
                probs.astype(BF), grad, over_queries, preferred_element_type=F32
            )
    for head in range(per):
        at = (per + head) * HEAD
        out_ref[:, at : at + HEAD] = (dk_ref[head] * (HEAD**-0.5)).astype(BF)
        at = (2 * per + head) * HEAD
        out_ref[:, at : at + HEAD] = dv_ref[head].astype(BF)


def vmem():
    return pl.BlockSpec(memory_space=pltpu.VMEM)


def attention_forward(ends, qkv, block):
    pack, columns = qkv.shape
    per = columns // (3 * HEAD)
    return pl.pallas_call(
        functools.partial(attention_forward_kernel, block, per),
        out_shape=jax.ShapeDtypeStruct((pack, per * HEAD), BF),
        in_specs=[pl.BlockSpec(memory_space=pltpu.SMEM), vmem()],
        out_specs=vmem(),
        compiler_params=pltpu.CompilerParams(vmem_limit_bytes=32 << 20),
        cost_estimate=pl.CostEstimate(
            flops=4 * per * pack * pack * HEAD, bytes_accessed=8 * pack * columns // 3, transcendentals=per * pack * pack
        ),
    )(ends, qkv)


def attention_backward(ends, qkv, grad, block):
    pack, columns = qkv.shape
    per = columns // (3 * HEAD)
    return pl.pallas_call(
        functools.partial(attention_backward_kernel, block, per),
        out_shape=jax.ShapeDtypeStruct((pack, columns), BF),
        in_specs=[pl.BlockSpec(memory_space=pltpu.SMEM), vmem(), vmem()],
        out_specs=vmem(),
        scratch_shapes=[pltpu.VMEM((per, pack, HEAD), F32)] * 2,
        compiler_params=pltpu.CompilerParams(vmem_limit_bytes=32 << 20),
        cost_estimate=pl.CostEstimate(
            flops=10 * per * pack * pack * HEAD, bytes_accessed=16 * pack * columns // 3, transcendentals=per * pack * pack
        ),
    )(ends, qkv, grad)


SPOT = 64
TAIL = 16
TILE = 512
WINDOW_STEP = (1, 2)
TAIL_STEP = (1, 2)
CHUNKS = (1, 2, 1, 1, 1)


def nt(a, b):
    return lax.dot_general(a, b, (((1,), (1,)), ((), ())), preferred_element_type=F32)


def nn(a, b):
    return jnp.dot(a, b, preferred_element_type=F32)


def slot_rows(slot_ref, k, first, count):
    row = slot_ref[k : k + 1, :]
    place = first + lax.broadcasted_iota(I32, (count, row.shape[1]), 0)
    return (place == row).astype(F32).astype(BF)


def slot_columns(info, capacity):
    column = info[:, SPOT : SPOT + 1]
    place = lax.broadcasted_iota(I32, (info.shape[0], capacity), 1).astype(F32)
    return (place == column).astype(F32).astype(BF)


def dispatch(slot_ref, block_refs, first, count):
    total = None
    for k, ref in enumerate(block_refs):
        part = nn(slot_rows(slot_ref, k, first, count), ref[...])
        total = part if total is None else total + part
    return total.astype(BF)


def from_either(which_ref, sources, body):
    @pl.when(which_ref[1] == 1)
    def _():
        body(*sources[0])

    @pl.when(which_ref[1] == 0)
    def _():
        body(*sources[1])


def moe_forward_kernel(members, experts, *refs):
    which_ref, slot_ref, info_ref, router_ref = refs[:4]
    h_refs, refs = refs[4 : 4 + members], refs[4 + members :]
    sources, (wsi_ref, wsd_ref), refs = (refs[:3], refs[3:6]), refs[6:8], refs[3:]
    rows_ref, g_ref, u_ref, a_ref, meta_ref, ret_ref, sg_ref, su_ref, sa_ref = refs[5:14]
    part_refs, (acc_ref, y_ref) = refs[14 : 14 + members], refs[14 + members :]
    step, last = pl.program_id(0), pl.num_programs(0) - 1
    capacity, tokens = rows_ref.shape[0], h_refs[0].shape[0]
    tiles = [slice(r, r + tokens) for r in range(0, capacity, tokens)]

    @pl.when(step == 0)
    def _():
        for r in tiles:
            rows_ref[r, :] = dispatch(slot_ref, h_refs, r.start, tokens)
            acc_ref[r, :] = jnp.zeros((tokens, acc_ref.shape[1]), F32)

    def units(wg_ref, wu_ref, wd_ref):
        for r in tiles:
            x = rows_ref[r, :]
            gate, up = nn(x, wg_ref[...]), nn(x, wu_ref[...])
            act = (gate * jax.nn.sigmoid(gate) * up).astype(BF)
            g_ref[r, :], u_ref[r, :], a_ref[r, :] = gate.astype(BF), up.astype(BF), act
            acc_ref[r, :] += nn(act, wd_ref[...])

    from_either(which_ref, sources, units)

    @pl.when(step == last)
    def _():
        for r in tiles:
            y_ref[r, :] = acc_ref[r, :].astype(BF)
        quarter = wsd_ref.shape[0]
        for k in range(members):
            t = slice(k * tokens, (k + 1) * tokens)
            h, info = h_refs[k][...], info_ref[t, :]
            lane = lax.broadcasted_iota(I32, info.shape, 1)
            logits = jnp.where(lane < experts, nn(h, router_ref[...]), -1e30)
            raised = jnp.exp(logits - jnp.max(logits, axis=-1, keepdims=True))
            probs = raised / jnp.sum(raised, axis=-1, keepdims=True)
            chosen = jnp.where(lane < experts, info, 0.0)
            picked = jnp.sum(probs * chosen, axis=-1, keepdims=True)
            here = jnp.sum(jnp.where(lane == which_ref[0], probs, 0.0), axis=-1, keepdims=True)
            weight = here / picked
            meta_ref[t, :] = jnp.where(lane == SPOT, weight, probs)
            gate, up = nn(h, wsi_ref[:, :quarter]), nn(h, wsi_ref[:, quarter:])
            act = (gate * jax.nn.sigmoid(gate) * up).astype(BF)
            sg_ref[t, :], su_ref[t, :], sa_ref[t, :] = gate.astype(BF), up.astype(BF), act
            back = nn(slot_columns(info, capacity), y_ref[...])
            ret_ref[t, :] = back.astype(BF)
            part_refs[k][...] = (weight * back + nn(act, wsd_ref[...])).astype(BF)


def act_grads(gate_low, up_low, grad_act):
    gate, up = gate_low.astype(F32), up_low.astype(F32)
    value, slope = silu_parts(gate)
    return (grad_act * up * slope).astype(BF), (grad_act * value).astype(BF)


def moe_backward_kernel(members, *refs):
    which_ref, slot_ref, info_ref, meta_ref = refs[:4]
    grad_refs, refs = refs[4 : 4 + members], refs[4 + members :]
    ret_ref, sources, refs = refs[0], (refs[1:4], refs[4:7]), refs[7:]
    g_ref, u_ref, sg_ref, su_ref, wsi_ref, wsd_ref = refs[:6]
    dy_ref, dg_ref, du_ref, dsg_ref, dsu_ref = refs[6:11]
    part_refs, (gated_ref, acc_ref) = refs[11 : 11 + members], refs[11 + members :]
    step, last = pl.program_id(0), pl.num_programs(0) - 1
    capacity, width = dy_ref.shape
    tokens = grad_refs[0].shape[0]
    tiles = [slice(r, r + tokens) for r in range(0, capacity, tokens)]

    @pl.when(step == 0)
    def _():
        for k in range(members):
            t = slice(k * tokens, (k + 1) * tokens)
            grad = grad_refs[k][...].astype(F32)
            weight = meta_ref[t, SPOT : SPOT + 1]
            gated_ref[k, :, :] = (weight * grad).astype(BF)
            product = grad * ret_ref[t, :].astype(F32)
            high = product.astype(BF)
            low = (product - high.astype(F32)).astype(BF)
            ones = jnp.ones((TAIL, width), BF)
            total = nt(ones, high) + nt(ones, low)
            high = total.astype(BF).astype(F32)
            row = lax.broadcasted_iota(I32, total.shape, 0)
            tail = jnp.where(row == 0, high, jnp.where(row == 1, total - high, 0.0))
            part_refs[k][tokens : tokens + TAIL, :] = jnp.zeros((TAIL, width), BF)
            part_refs[k][tokens : tokens + TAIL, :tokens] = tail.astype(BF)
        for r in tiles:
            dy_ref[r, :] = dispatch(slot_ref, [gated_ref.at[k] for k in range(members)], r.start, tokens)
            acc_ref[r, :] = jnp.zeros((tokens, width), F32)

    def units(wg_ref, wu_ref, wd_ref):
        for r in tiles:
            dg, du = act_grads(g_ref[r, :], u_ref[r, :], nt(dy_ref[r, :], wd_ref[...]))
            dg_ref[r, :], du_ref[r, :] = dg, du
            acc_ref[r, :] += nt(dg, wg_ref[...]) + nt(du, wu_ref[...])

    from_either(which_ref, sources, units)

    @pl.when(step == last)
    def _():
        rows = acc_ref[...].astype(BF)
        quarter = wsd_ref.shape[0]
        for k in range(members):
            t = slice(k * tokens, (k + 1) * tokens)
            dsg, dsu = act_grads(sg_ref[t, :], su_ref[t, :], nt(grad_refs[k][...], wsd_ref[...]))
            dsg_ref[t, :], dsu_ref[t, :] = dsg, dsu
            back = nt(dsg, wsi_ref[:, :quarter]) + nt(dsu, wsi_ref[:, quarter:])
            back = back + nn(slot_columns(info_ref[t, :], capacity), rows)
            part_refs[k][:tokens, :] = back.astype(BF)


def whole_block(*shape):
    return pl.BlockSpec(shape, lambda i, which: (0,) * len(shape), pipeline_mode=pl.Buffered(1))


def expert_specs(width):
    steps = FF // TILE

    def tiles(own):
        def at(i, which):
            return i * (which[1] if own else 1 - which[1])

        return [
            pl.BlockSpec((width, TILE), lambda i, which: (0, at(i, which))),
            pl.BlockSpec((width, TILE), lambda i, which: (0, steps + at(i, which))),
            pl.BlockSpec((TILE, width), lambda i, which: (at(i, which), 0)),
        ]

    return tiles(True) + tiles(False)


def expert_args(experts):
    return [w for w_in, w_down in experts for w in (w_in, w_in, w_down)]


def moe_call(kernel, shapes, in_specs, out_tiled, scratch, args, work):
    whole = [whole_block(*shape) for shape, _ in shapes]
    tiled = pl.BlockSpec((shapes[0][0][0], TILE), lambda i, which: (0, i))
    return pl.pallas_call(
        kernel,
        out_shape=[jax.ShapeDtypeStruct(*shape) for shape in shapes],
        grid_spec=pltpu.PrefetchScalarGridSpec(
            num_scalar_prefetch=1,
            grid=(FF // TILE,),
            in_specs=in_specs,
            out_specs=whole[:1] + [tiled] * out_tiled + whole[1 + out_tiled :],
            scratch_shapes=scratch,
        ),
        compiler_params=pltpu.CompilerParams(vmem_limit_bytes=56 << 20),
        cost_estimate=pl.CostEstimate(flops=work, bytes_accessed=30 << 20, transcendentals=1 << 20),
    )(*args)


def moe_work(width, capacity, everyone, quarter):
    return 2 * width * (capacity * (3 * FF + 2 * everyone) + 3 * everyone * quarter)


def moe_forward(which, slot, info, w_small, blocks, experts, w_sin, w_sdown, capacity, count):
    members, (tokens, width), quarter = len(blocks), blocks[0].shape, w_sdown.shape[0]
    everyone = members * tokens
    shapes = [((capacity, width), BF)] + [((capacity, FF), BF)] * 3
    shapes += [((everyone, 128), F32), ((everyone, width), BF)] + [((everyone, quarter), BF)] * 3
    shapes += [((tokens, width), BF)] * members
    in_specs = [whole_block(members, tokens), whole_block(everyone, 128), whole_block(width, 128)]
    in_specs += [whole_block(tokens, width)] * members + expert_specs(width)
    in_specs += [whole_block(width, 2 * quarter), whole_block(quarter, width)]
    return moe_call(
        functools.partial(moe_forward_kernel, members, count),
        shapes,
        in_specs,
        3,
        [pltpu.VMEM((capacity, width), F32), pltpu.VMEM((capacity, width), BF)],
        (which, slot, info, w_small, *blocks, *expert_args(experts), w_sin, w_sdown),
        moe_work(width, capacity, everyone, quarter),
    )


def moe_backward(which, slot, info, meta, blocks, ret, experts, gate, up, sg, su, w_sin, w_sdown):
    members, (tokens, width), quarter = len(blocks), blocks[0].shape, w_sdown.shape[0]
    everyone, capacity = members * tokens, gate.shape[0]
    shapes = [((capacity, width), BF)] + [((capacity, FF), BF)] * 2
    shapes += [((everyone, quarter), BF)] * 2 + [((tokens + TAIL, width), BF)] * members
    in_specs = [whole_block(members, tokens), whole_block(everyone, 128), whole_block(everyone, 128)]
    in_specs += [whole_block(tokens, width)] * members + [whole_block(everyone, width)] + expert_specs(width)
    in_specs += [pl.BlockSpec((capacity, TILE), lambda i, which: (0, i))] * 2
    in_specs += [whole_block(everyone, quarter)] * 2
    in_specs += [whole_block(width, 2 * quarter), whole_block(quarter, width)]
    return moe_call(
        functools.partial(moe_backward_kernel, members),
        shapes,
        in_specs,
        2,
        [pltpu.VMEM((members, tokens, width), BF), pltpu.VMEM((capacity, width), F32)],
        (which, slot, info, meta, *blocks, ret, *expert_args(experts), gate, up, sg, su, w_sin, w_sdown),
        moe_work(width, capacity, everyone, quarter),
    )


def after(values, *others):
    return lax.optimization_barrier((values, others))[0]


class Weights:
    def __init__(self, core, members, gains, w_qkv, w_out, w_router, *rest):
        self.core, self.members, self.width = core, members, w_out.shape[1]
        self.experts = w_router.shape[1]
        rows, extra = w_qkv.shape[0], self.experts + 2
        small = jnp.concatenate([w_router, gains.T, jnp.zeros((rows, 128 - extra), BF)], axis=1)
        self.first_shares = self.shares(jnp.concatenate([w_qkv, small], axis=1))
        self.out_shares = self.shares(w_out)
        self.w_sin, self.w_sdown, self.w_ein, self.w_edown = rest

    def both(self, mine):
        other = swap_cores(mine)
        return by_core(self.core, mine, other), by_core(self.core, other, mine)

    def shares(self, shard):
        mine, theirs = half_of(shard, self.core), half_of(shard, 1 - self.core)
        other = swap_cores(theirs)
        return by_core(self.core, mine, other), by_core(self.core, other, mine)

    def both_halves(self, full):
        blocks, rows, columns = full.shape
        other = swap_cores(full)
        halves = [by_core(self.core, full, other), by_core(self.core, other, full)]
        return jnp.stack(halves, axis=1).reshape(blocks * 2 * rows, columns)

    def permuted(self, part):
        me, blocks = lax.axis_index(EXP), jnp.stack(gather_blocks(part, self.members))
        return jnp.concatenate(
            [lax.dynamic_slice_in_dim(blocks, me ^ j, 1, 0) for j in range(self.members)]
        )

    def split_first(self, first):
        at = 3 * self.width
        small = first[:, at : at + 128]
        return first[:, :at], small, small[:, self.experts : self.experts + 2].T.astype(F32)

    def shared_in(self, w_sin):
        me, quarter = lax.axis_index(EXP), FF // self.members
        blocks = []
        for k in range(self.members):
            at = (me ^ k) * quarter
            parts = [lax.dynamic_slice_in_dim(w_sin, start + at, quarter, 1) for start in (0, FF)]
            blocks.append(jnp.concatenate(parts, axis=1))
        blocks = jnp.stack(scatter_blocks(blocks))
        return jnp.concatenate([lax.dynamic_index_in_dim(blocks, me ^ j, 0, False) for j in range(self.members)])


def add_low(a, b):
    return (a.astype(F32) + b.astype(F32)).astype(BF)


class LineSums:
    def __init__(self):
        lane = lax.axis_index(DP)
        self.middle = (lane == 1) | (lane == 2)
        self.now, self.waiting, self.flights, self.done = 0, [], [], {}

    def add(self, section, name, chunks):
        self.waiting += [((section, name, i), chunk) for i, chunk in enumerate(chunks)]

    def busy(self):
        return self.waiting or self.flights

    def step(self, main, count=WINDOW_STEP[0], steps=WINDOW_STEP[1]):
        self.now += 1
        landed = [flight for flight in self.flights if flight[0] <= self.now]
        self.flights = [flight for flight in self.flights if flight[0] > self.now]
        fresh, self.waiting = self.waiting[:count], self.waiting[count:]
        tied = (main, [flight[3:] for flight in landed], [item[1] for item in fresh])
        main, states, chunks = lax.optimization_barrier(tied)

        def launch(stage, key, value, axis, pairs, wait):
            got = lax.ppermute(value, axis, pairs)
            self.flights.append((self.now + wait, stage, key, value, got))

        for (_, stage, key, *_), (value, got) in zip(landed, states):
            if stage == 0:
                launch(1, key, add_low(value, got), DP, [(1, 2), (2, 1)], steps)
            elif stage == 1:
                launch(2, key, add_low(value, got), DP, [(1, 0), (2, 3)], steps)
            elif stage == 2:
                pair = (1, 0) if key[0] == 0 else (0, 1)
                launch(3, key, jnp.where(self.middle, value, got), SEC, [pair], 1)
            else:
                self.done[key] = (value, got)
        for (key, _), chunk in zip(fresh, chunks):
            launch(0, key, chunk, DP, [(0, 1), (3, 2)], steps)
        return main

    def result(self, section, name):
        keys = sorted(key for key in self.done if key[:2] == (section, name))
        return [self.done[key] for key in keys]


def cut(v, count):
    rows = v.shape[0] // count
    return [v[i * rows : (i + 1) * rows] for i in range(count)]


def to_heads(v, lanes, parts):
    tokens, columns = v.shape
    per = columns // (parts * lanes)
    split = v.reshape(tokens, parts, lanes, per).transpose(2, 0, 1, 3).reshape(lanes, tokens, parts * per)
    return a2a(split, DP).reshape(lanes * tokens, parts * per)


def to_tokens(v, lanes, parts):
    pack, columns = v.shape
    tokens, per = pack // lanes, columns // parts
    got = a2a(v.reshape(lanes, tokens, columns), DP).reshape(lanes, tokens, parts, per)
    return got.transpose(1, 2, 0, 3).reshape(tokens, lanes * columns)


def add_blocks(first, blocks):
    return functools.reduce(jnp.add, [block.astype(F32) for block in blocks], first)


def layer_mlp(middle, context, weights, beside=None):
    gain, w_small, w_sin, w_sdown, experts, which = weights
    me, slot, info, capacity, count = context
    members = slot.shape[0]
    hidden, scale = norm_apply(middle, gain)
    blocks = gather_blocks(hidden, members)
    out = moe_forward(which, slot, info, w_small, blocks, experts, w_sin, w_sdown, capacity, count)
    if beside is not None:
        out = beside(out)
    parts = scatter_blocks(out[9:])
    return add_blocks(middle, parts), (scale, hidden, blocks, *out[:9])


def mlp_backward(grad_blocks, middle, saved, context, weights, sums, ready, kernel_done):
    gain, w_small, w_sin, w_sdown, expert_weights, which = weights
    me, slot, info, capacity, experts = context
    scale, hidden, blocks, rows, gate, up, act, meta, ret, sg, su, sact = saved
    members, (tokens, width) = len(blocks), middle.shape
    out = moe_backward(
        which, slot, info, meta, grad_blocks, ret, expert_weights, gate, up, sg, su, w_sin, w_sdown
    )
    out = sums.step(kernel_done(out))
    dy, dg, du, dsg, dsu = out[:5]
    parts = scatter_blocks(out[5:])
    ready((rows, act, dy, dg, du), (blocks, sact, grad_blocks, dsg, dsu))
    parts = sums.step(parts)
    dh2 = add_blocks(jnp.zeros(middle.shape, F32), [part[:tokens] for part in parts])
    tails = [part[tokens : tokens + 2, :tokens].astype(F32) for part in parts]
    column = jnp.arange(experts, dtype=I32)[None, :]
    dgates = sum(
        jnp.where(column == (me ^ k), (tail[0] + tail[1])[:, None], 0.0) for k, tail in enumerate(tails)
    )
    router, chosen = meta[:tokens, :experts], info[:tokens, :experts]
    picked = jnp.sum(router * chosen, axis=-1, keepdims=True)
    inner = jnp.sum(dgates * router * chosen, axis=-1, keepdims=True) / picked
    dprob = chosen * (dgates - inner) / picked
    dlogits = (router * (dprob - jnp.sum(router * dprob, axis=-1, keepdims=True))).astype(BF)
    dh2 = dh2 + mm(dlogits, w_small[:, :experts], 1, 1)
    dmiddle_norm, dgain = norm_backward(dh2, middle, scale, gain)
    dmiddle = grad_blocks[0].astype(F32) + dmiddle_norm
    return dmiddle, dgain, dlogits


def halves(rows_of, grads, core):
    send = mm(half_of(rows_of, 1 - core, 1), grads, 0, 0, out=BF)
    keep = mm(half_of(rows_of, core, 1), grads, 0, 0)
    return (keep + swap_cores(send).astype(F32)).astype(BF)


def halves_by_member(rows_of, grads, core, members):
    split = rows_of.reshape(rows_of.shape[0], members, 2, -1)

    def side(which):
        return lax.dynamic_index_in_dim(split, which, 2, False).reshape(rows_of.shape[0], -1)

    send = mm(side(1 - core), grads, 0, 0, out=BF)
    keep = mm(side(core), grads, 0, 0)
    return (keep + swap_cores(send).astype(F32)).astype(BF).reshape(members, -1, grads.shape[1])


def expert_grads(terms, core):
    rows, act, dy, dg, du = terms
    g_in = jnp.concatenate([halves(rows, dg, core), halves(rows, du, core)], axis=1)
    return halves(act, dy, core), g_in


def shared_grads(terms, core):
    blocks, sact, grad_blocks, dsg, dsu = terms
    members = len(blocks)
    hidden_all, grad_all = jnp.concatenate(blocks), jnp.concatenate(grad_blocks)
    g_in = halves_by_member(hidden_all, jnp.concatenate([dsg, dsu], axis=1), core, members)
    return halves(sact, grad_all, core), a2a(g_in, EXP)


def dense_grads(terms, core, members):
    hidden_one, dqkv, mixed, dattn, hidden_two, dlogits, dgains = terms
    width, experts = hidden_one.shape[1], dlogits.shape[1]
    small = jnp.concatenate(
        [mm(hidden_two, dlogits, 0, 0), jnp.stack(dgains, axis=1), jnp.zeros((width, 126 - experts), F32)],
        axis=1,
    )
    split = small.reshape(members, 2, -1, 128)
    send = lax.dynamic_index_in_dim(split, 1 - core, 1, False).astype(BF)
    keep = lax.dynamic_index_in_dim(split, core, 1, False)
    small = (keep + swap_cores(send).astype(F32)).astype(BF)
    g_out = halves_by_member(mixed, dattn, core, members)
    g_qkv = halves_by_member(hidden_one, dqkv, core, members)
    return jnp.concatenate([g_qkv, g_out, small], axis=2)


def member_sum(parts):
    return jnp.sum(parts.astype(F32), axis=0).astype(BF)


def local(
    inputs, cotangent, lengths, deal, routes, order, gains, w_qkv, w_out, w_router, w_shared_in, w_shared_down,
    w_expert_in, w_expert_down,
):
    core, me = lax.axis_index(SEC), lax.axis_index(EXP)
    members, lanes = lax.axis_size(EXP), lax.axis_size(DP)
    batches, _, tokens, width = inputs.shape
    experts = w_router.shape[2]
    assert batches == lax.axis_size(SEC) == 2 and w_expert_in.shape[1] == 1 and experts == members
    w = Weights(
        core, members, gains[0], w_qkv[0], w_out[0], w_router[0], w_shared_in[0], w_shared_down[0],
        w_expert_in[0, 0], w_expert_down[0, 0],
    )
    first_low = lax.dynamic_index_in_dim(inputs[:, 0], core, 0, False)
    grad_low = lax.dynamic_index_in_dim(cotangent[:, 0], core, 0, False)
    row = lax.dynamic_index_in_dim(deal, core * members + me, 0, False)
    ends = jnp.cumsum(lax.dynamic_index_in_dim(lengths, row, 0, False))[:-1].astype(I32)
    qkv_0, w_small_0, gains_0 = w.split_first(w.both_halves(w.permuted(w.first_shares[0])))
    current_0 = first_low.astype(F32)
    hidden_0, scale_0 = norm_apply(current_0, gains_0[0])
    projected = mm(hidden_0, qkv_0, out=BF)
    pairs = lax.dynamic_index_in_dim(routes[:, 0], core, 0, False).reshape(-1)
    places = lax.dynamic_index_in_dim(order[:, 0], core, 0, False)
    same = pairs[:, None] == pairs[None, :]
    rank = jnp.sum((same & (places[None, :] < places[:, None])).astype(I32), axis=1)
    code = jnp.stack(gather_blocks(after(pairs * (2 * tokens) + rank, projected), members))
    owner = me ^ jnp.arange(members, dtype=I32)
    pairs_all, rank_all = code // (2 * tokens), code % (2 * tokens)
    onehot = (pairs_all[:, :, None] == jnp.arange(experts, dtype=I32)).astype(I32)
    counts = jnp.sum(onehot, axis=1)
    lower = (owner[None, :] < owner[:, None]).astype(I32)
    before = jnp.sum(lower[:, :, None] * counts[None], axis=1)
    place = jnp.sum(onehot * before[:, None, :], axis=2) + rank_all
    capacity = 2 * tokens * members // experts
    slot = jnp.where((pairs_all == me) & (place < capacity), place, -1)
    slot = jnp.max(slot.reshape(members, tokens, 2), axis=2)
    column = jnp.arange(128, dtype=I32)[None, :]
    named = pairs_all.reshape(members * tokens, 2)
    chosen = (named[:, :1] == column) | (named[:, 1:] == column)
    info = jnp.where(column == SPOT, slot.reshape(-1, 1).astype(F32), chosen.astype(F32))

    w_out_0 = w.both_halves(w.permuted(after(w.out_shares[0], projected)))
    shared_in = w.shared_in(after(w.w_sin, projected))
    shared = (shared_in, w.w_sdown)
    shared = (shared, (swap_cores(shared_in), swap_cores(w.w_sdown)))
    expert_weights = ((w.w_ein, w.w_edown), (swap_cores(w.w_ein), swap_cores(w.w_edown)))
    which = [jnp.stack([me, (core == s).astype(I32)]) for s in range(2)]
    heads_0 = to_heads(projected, lanes, 3)
    heads_0, slot, info, w_out_0 = lax.optimization_barrier((heads_0, slot, info, w_out_0))
    context = (me, slot, info, capacity, experts)
    later = jnp.concatenate([w.first_shares[1], w.out_shares[1]], axis=1)
    mixed_0, shared = lax.optimization_barrier((attention_forward(ends, heads_0, tokens), shared))
    mixed_0 = to_tokens(mixed_0, lanes, 1)
    shared_first = [by_core(core, mine, other) for mine, other in zip(*shared)]
    mixed_0, shared_first = lax.optimization_barrier((mixed_0, shared_first))
    shared_second = [by_core(core, other, mine) for mine, other in zip(*shared)]
    middle_0 = current_0 + mm(mixed_0, w_out_0)
    gathered = []

    def land(out):
        out, full = lax.optimization_barrier((out, lax.all_gather(after(later, middle_0), EXP)))
        gathered.append(full)
        return out

    mlp_0 = (gains_0[1], w_small_0, *shared_first, expert_weights, which[0])
    out_0, saved_0 = layer_mlp(middle_0, context, mlp_0, land)
    dense_1 = w.both_halves(gathered[0])
    low_0, dense_1, shared_second = lax.optimization_barrier((out_0.astype(BF), dense_1, shared_second))
    qkv_1, w_small_1, gains_1 = w.split_first(dense_1)
    w_out_1 = dense_1[:, 3 * width + 128 :]
    current_1 = low_0.astype(F32)
    hidden_1, scale_1 = norm_apply(current_1, gains_1[0])
    projected = mm(hidden_1, qkv_1, out=BF)
    grad_blocks = gather_blocks(after(grad_low, projected), members)
    heads_1 = to_heads(projected, lanes, 3)
    heads_1, grad_blocks = lax.optimization_barrier((heads_1, grad_blocks))
    mixed_1 = to_tokens(attention_forward(ends, heads_1, tokens), lanes, 1)
    middle_1 = current_1 + mm(mixed_1, w_out_1)
    mlp_1 = (gains_1[1], w_small_1, *shared_second, expert_weights, which[1])
    out_1, saved_1 = layer_mlp(middle_1, context, mlp_1)
    low_1 = out_1.astype(BF)

    sums = LineSums()

    def backward(section, grad_blocks, current, hidden, scale, heads, mixed, middle, saved, gain, w_qkv_s, w_out_s, mlp, beside=None):
        shared = []

        def kernel_done(out):
            if beside is None:
                return out
            out, parts = lax.optimization_barrier((out, a2a(beside, EXP)))
            sums.add(1 - section, 4, [member_sum(parts)])
            return out

        def ready(terms, shared_terms):
            down, ein = expert_grads(terms, core)
            sums.add(section, 0, cut(down, CHUNKS[0]))
            sums.add(section, 1, cut(ein, CHUNKS[1]))
            shared.append(shared_terms)

        dmiddle, dgain_two, dlogits = mlp_backward(
            grad_blocks, middle, saved, context, mlp, sums, ready, kernel_done
        )
        dattn = dmiddle.astype(BF)
        dheads = to_heads(mm(dattn, w_out_s, 1, 1, out=BF), lanes, 1)
        g_sdown, g_sin = shared_grads(shared[0], core)
        sums.add(section, 2, [g_sdown])
        sums.add(section, 3, [g_sin.reshape(-1, g_sin.shape[2])])
        dheads = sums.step(dheads)
        dheads = sums.step(attention_backward(ends, heads, dheads, tokens))
        dqkv = sums.step(to_tokens(dheads, lanes, 3))
        dinput, dgain_one = norm_backward(mm(dqkv, w_qkv_s, 1, 1), current, scale, gain)
        dense = (hidden, dqkv, mixed, dattn, saved[1], dlogits, (dgain_one, dgain_two))
        return dmiddle + dinput, dense_grads(dense, core, members)

    grad_1, dense_1 = backward(
        1, grad_blocks, current_1, hidden_1, scale_1, heads_1, mixed_1, middle_1, saved_1, gains_1[0], qkv_1,
        w_out_1, mlp_1,
    )
    grad_blocks, dense_1 = lax.optimization_barrier((gather_blocks(grad_1.astype(BF), members), dense_1))
    grad_blocks = sums.step(grad_blocks)
    grad_0, dense_0 = backward(
        0, grad_blocks, current_0, hidden_0, scale_0, heads_0, mixed_0, middle_0, saved_0, gains_0[0], qkv_0,
        w_out_0, mlp_0, dense_1,
    )
    sums.add(0, 4, [member_sum(a2a(dense_0, EXP))])
    quarter = FF // members

    def by_columns(half):
        blocks = half.reshape(members, -1, 2 * quarter)
        return jnp.concatenate(
            [blocks[j][:, at : at + quarter] for at in (0, quarter) for j in range(members)], axis=1
        )

    def whole(name):
        own_0, got_0 = zip(*sums.result(0, name))
        own_1, got_1 = zip(*sums.result(1, name))
        pairs = zip(own_0 + got_0, got_1 + own_1)
        parts = [by_core(core, a, b) for a, b in pairs]
        return jnp.concatenate([by_columns(v) if name == 3 else v for v in parts]).astype(F32)

    def complete(name):
        return all(len(sums.result(section, name)) == CHUNKS[name] for section in range(2))

    results = {}
    while sums.busy():
        results = sums.step(results, *TAIL_STEP)
        results.update({name: whole(name) for name in range(5) if name not in results and complete(name)})

    def to_section(of_0, of_1):
        mine = by_core(core, of_0, of_1)
        other = swap_cores(by_core(core, of_1, of_0))
        both = jnp.stack([by_core(core, mine, other), by_core(core, other, mine)])
        return both[None, :, None]

    down, ein, sdown, sin, dense = [results[name] for name in range(5)]
    at = 4 * width
    return (
        to_section(low_0, low_1),
        to_section(grad_0, grad_1),
        dense[:, at + experts : at + experts + 2].T[None],
        dense[None, :, : 3 * width],
        dense[None, :, 3 * width : at],
        dense[None, :, at : at + experts],
        sin[None],
        sdown[None],
        ein[None, None],
        down[None, None],
    )


def solution(mesh):
    tokens = P(None, EXP, DP, None)
    dense = P(SEC, EXP, None)
    expert = P(SEC, EXP, None, None)
    both = P(SEC, None, EXP, DP, None)
    gains = P(SEC, None, EXP)
    return jax.shard_map(
        local,
        mesh=mesh,
        in_specs=(tokens, tokens, P(), P(), tokens, P(None, EXP, DP), gains)
        + (dense,) * 5
        + (expert,) * 2,
        out_specs=(both, both, gains) + (dense,) * 5 + (expert,) * 2,
        check_vma=False,
    )
```

```python
import functools
import jax
import jax.numpy as jnp
from jax import lax
from jax.experimental import pallas as pl
from jax.experimental.pallas import tpu as pltpu
from jax.sharding import PartitionSpec as P

HEADS = 12
HEAD = 64
FF = 2048
EPS = 1e-06

SEC, DP, EXP = "section", "dp", "expert"
BF, F32, I32 = jnp.bfloat16, jnp.float32, jnp.int32
SWAP = [(0, 1), (1, 0)]


def mm(a, b, ca=1, cb=0, out=F32):
    r = lax.dot_general(a, b, (((ca,), (cb,)), ((), ())), preferred_element_type=F32)
    return r.astype(out)


def swap_cores(v):
    return lax.ppermute(v, SEC, SWAP)


def a2a(v, axis):
    return lax.all_to_all(v, axis, split_axis=0, concat_axis=0, tiled=True)


def gather(v, axis):
    return lax.all_gather(v, axis, axis=0, tiled=True)


def xor_pairs(count, k):
    return [(i, i ^ k) for i in range(count)]


def gather_blocks(v, members):
    return [v] + [lax.ppermute(v, EXP, xor_pairs(members, k)) for k in range(1, members)]


def scatter_blocks(blocks):
    count = len(blocks)
    return [blocks[0]] + [lax.ppermute(blocks[k], EXP, xor_pairs(count, k)) for k in range(1, count)]


def half_of(v, which, axis=0):
    size = v.shape[axis] // 2
    return lax.dynamic_slice_in_dim(v, which * size, size, axis)


def by_core(core, first, second):
    return jnp.where(core == 0, first, second)


def norm_apply(values, gain):
    scale = lax.rsqrt(jnp.mean(values * values, axis=-1, keepdims=True) + EPS)
    return (values * scale * gain).astype(BF), scale


def norm_backward(grad_hidden, values, scale, gain):
    normed = values * scale
    grad_gain = jnp.sum(grad_hidden * normed, axis=0)
    grad_normed = grad_hidden * gain
    grad_values = scale * (
        grad_normed - normed * jnp.mean(grad_normed * normed, axis=-1, keepdims=True)
    )
    return grad_values, grad_gain


def silu(v):
    return v * jax.nn.sigmoid(v)


def silu_parts(v):
    logistic = jax.nn.sigmoid(v)
    return v * logistic, logistic * (1.0 + v * (1.0 - logistic))


def block_mask(ends_ref, first_row, rows, cols):
    q = first_row + lax.broadcasted_iota(I32, (rows, cols), 0)
    k = lax.broadcasted_iota(I32, (rows, cols), 1)
    start = jnp.zeros((rows, cols), I32)
    for i in range(ends_ref.shape[0]):
        end = ends_ref[i]
        start = jnp.where(q >= end, end, start)
    return (k <= q) & (k >= start)


def head_slices(ref, rows, head, per, parts):
    return [ref[rows, (part * per + head) * HEAD : (part * per + head + 1) * HEAD] for part in parts]


def block_probs(q, k, mask):
    scores = lax.dot_general(q, k, (((1,), (1,)), ((), ())), preferred_element_type=F32)
    scores = jnp.where(mask, scores * (HEAD**-0.5), -1e30)
    raised = jnp.exp(scores - jnp.max(scores, axis=-1, keepdims=True))
    return raised / jnp.sum(raised, axis=-1, keepdims=True)


def attention_forward_kernel(block, per, ends_ref, qkv_ref, out_ref):
    pack = qkv_ref.shape[0]
    for i in range(pack // block):
        rows, reach = slice(i * block, (i + 1) * block), slice(0, (i + 1) * block)
        mask = block_mask(ends_ref, i * block, block, (i + 1) * block)
        for head in range(per):
            (q,) = head_slices(qkv_ref, rows, head, per, (0,))
            k, v = head_slices(qkv_ref, reach, head, per, (1, 2))
            probs = block_probs(q, k, mask).astype(BF)
            mixed = jnp.dot(probs, v, preferred_element_type=F32)
            out_ref[rows, head * HEAD : (head + 1) * HEAD] = mixed.astype(BF)


def attention_backward_kernel(block, per, ends_ref, qkv_ref, grad_ref, out_ref, dk_ref, dv_ref):
    pack = qkv_ref.shape[0]
    dk_ref[...] = jnp.zeros_like(dk_ref)
    dv_ref[...] = jnp.zeros_like(dv_ref)
    for i in range(pack // block):
        rows, reach = slice(i * block, (i + 1) * block), slice(0, (i + 1) * block)
        mask = block_mask(ends_ref, i * block, block, (i + 1) * block)
        for head in range(per):
            (q,) = head_slices(qkv_ref, rows, head, per, (0,))
            k, v = head_slices(qkv_ref, reach, head, per, (1, 2))
            grad = grad_ref[rows, head * HEAD : (head + 1) * HEAD]
            probs = block_probs(q, k, mask)
            dprobs = lax.dot_general(grad, v, (((1,), (1,)), ((), ())), preferred_element_type=F32)
            delta = jnp.sum(probs * dprobs, axis=-1, keepdims=True)
            dscores = (probs * (dprobs - delta)).astype(BF)
            dq = jnp.dot(dscores, k, preferred_element_type=F32) * (HEAD**-0.5)
            out_ref[rows, head * HEAD : (head + 1) * HEAD] = dq.astype(BF)
            over_queries = (((0,), (0,)), ((), ()))
            dk_ref[head, reach, :] += lax.dot_general(
                dscores, q, over_queries, preferred_element_type=F32
            )
            dv_ref[head, reach, :] += lax.dot_general(
                probs.astype(BF), grad, over_queries, preferred_element_type=F32
            )
    for head in range(per):
        at = (per + head) * HEAD
        out_ref[:, at : at + HEAD] = (dk_ref[head] * (HEAD**-0.5)).astype(BF)
        at = (2 * per + head) * HEAD
        out_ref[:, at : at + HEAD] = dv_ref[head].astype(BF)


def vmem():
    return pl.BlockSpec(memory_space=pltpu.VMEM)


def attention_forward(ends, qkv, block):
    pack, columns = qkv.shape
    per = columns // (3 * HEAD)
    return pl.pallas_call(
        functools.partial(attention_forward_kernel, block, per),
        out_shape=jax.ShapeDtypeStruct((pack, per * HEAD), BF),
        in_specs=[pl.BlockSpec(memory_space=pltpu.SMEM), vmem()],
        out_specs=vmem(),
        compiler_params=pltpu.CompilerParams(vmem_limit_bytes=32 << 20),
        cost_estimate=pl.CostEstimate(
            flops=4 * per * pack * pack * HEAD, bytes_accessed=8 * pack * columns // 3, transcendentals=per * pack * pack
        ),
    )(ends, qkv)


def attention_backward(ends, qkv, grad, block):
    pack, columns = qkv.shape
    per = columns // (3 * HEAD)
    return pl.pallas_call(
        functools.partial(attention_backward_kernel, block, per),
        out_shape=jax.ShapeDtypeStruct((pack, columns), BF),
        in_specs=[pl.BlockSpec(memory_space=pltpu.SMEM), vmem(), vmem()],
        out_specs=vmem(),
        scratch_shapes=[pltpu.VMEM((per, pack, HEAD), F32)] * 2,
        compiler_params=pltpu.CompilerParams(vmem_limit_bytes=32 << 20),
        cost_estimate=pl.CostEstimate(
            flops=10 * per * pack * pack * HEAD, bytes_accessed=16 * pack * columns // 3, transcendentals=per * pack * pack
        ),
    )(ends, qkv, grad)


SPOT = 64
TAIL = 16
TILE = 512
WINDOW_STEP = (1, 2)
TAIL_STEP = (1, 2)
CHUNKS = (1, 2, 1, 1, 1)


def nt(a, b):
    return lax.dot_general(a, b, (((1,), (1,)), ((), ())), preferred_element_type=F32)


def nn(a, b):
    return jnp.dot(a, b, preferred_element_type=F32)


def slot_rows(slot_ref, k, first, count):
    row = slot_ref[k : k + 1, :]
    place = first + lax.broadcasted_iota(I32, (count, row.shape[1]), 0)
    return (place == row).astype(F32).astype(BF)


def slot_columns(info, capacity):
    column = info[:, SPOT : SPOT + 1]
    place = lax.broadcasted_iota(I32, (info.shape[0], capacity), 1).astype(F32)
    return (place == column).astype(F32).astype(BF)


def dispatch(slot_ref, block_refs, first, count):
    total = None
    for k, ref in enumerate(block_refs):
        part = nn(slot_rows(slot_ref, k, first, count), ref[...])
        total = part if total is None else total + part
    return total.astype(BF)


def from_either(which_ref, sources, body):
    @pl.when(which_ref[1] == 1)
    def _():
        body(*sources[0])

    @pl.when(which_ref[1] == 0)
    def _():
        body(*sources[1])


def moe_forward_kernel(members, experts, *refs):
    which_ref, slot_ref, info_ref, router_ref = refs[:4]
    h_refs, refs = refs[4 : 4 + members], refs[4 + members :]
    sources, (wsi_ref, wsd_ref), refs = (refs[:3], refs[3:6]), refs[6:8], refs[3:]
    rows_ref, g_ref, u_ref, a_ref, meta_ref, ret_ref, sg_ref, su_ref, sa_ref = refs[5:14]
    part_refs, (acc_ref, y_ref) = refs[14 : 14 + members], refs[14 + members :]
    step, last = pl.program_id(0), pl.num_programs(0) - 1
    capacity, tokens = rows_ref.shape[0], h_refs[0].shape[0]
    tiles = [slice(r, r + tokens) for r in range(0, capacity, tokens)]

    @pl.when(step == 0)
    def _():
        for r in tiles:
            rows_ref[r, :] = dispatch(slot_ref, h_refs, r.start, tokens)
            acc_ref[r, :] = jnp.zeros((tokens, acc_ref.shape[1]), F32)

    def units(wg_ref, wu_ref, wd_ref):
        for r in tiles:
            x = rows_ref[r, :]
            gate, up = nn(x, wg_ref[...]), nn(x, wu_ref[...])
            act = (gate * jax.nn.sigmoid(gate) * up).astype(BF)
            g_ref[r, :], u_ref[r, :], a_ref[r, :] = gate.astype(BF), up.astype(BF), act
            acc_ref[r, :] += nn(act, wd_ref[...])

    from_either(which_ref, sources, units)

    @pl.when(step == last)
    def _():
        for r in tiles:
            y_ref[r, :] = acc_ref[r, :].astype(BF)
        quarter = wsd_ref.shape[0]
        for k in range(members):
            t = slice(k * tokens, (k + 1) * tokens)
            h, info = h_refs[k][...], info_ref[t, :]
            lane = lax.broadcasted_iota(I32, info.shape, 1)
            logits = jnp.where(lane < experts, nn(h, router_ref[...]), -1e30)
            raised = jnp.exp(logits - jnp.max(logits, axis=-1, keepdims=True))
            probs = raised / jnp.sum(raised, axis=-1, keepdims=True)
            chosen = jnp.where(lane < experts, info, 0.0)
            picked = jnp.sum(probs * chosen, axis=-1, keepdims=True)
            here = jnp.sum(jnp.where(lane == which_ref[0], probs, 0.0), axis=-1, keepdims=True)
            weight = here / picked
            meta_ref[t, :] = jnp.where(lane == SPOT, weight, probs)
            gate, up = nn(h, wsi_ref[:, :quarter]), nn(h, wsi_ref[:, quarter:])
            act = (gate * jax.nn.sigmoid(gate) * up).astype(BF)
            sg_ref[t, :], su_ref[t, :], sa_ref[t, :] = gate.astype(BF), up.astype(BF), act
            back = nn(slot_columns(info, capacity), y_ref[...])
            ret_ref[t, :] = back.astype(BF)
            part_refs[k][...] = (weight * back + nn(act, wsd_ref[...])).astype(BF)


def act_grads(gate_low, up_low, grad_act):
    gate, up = gate_low.astype(F32), up_low.astype(F32)
    value, slope = silu_parts(gate)
    return (grad_act * up * slope).astype(BF), (grad_act * value).astype(BF)


def moe_backward_kernel(members, *refs):
    which_ref, slot_ref, info_ref, meta_ref = refs[:4]
    grad_refs, refs = refs[4 : 4 + members], refs[4 + members :]
    ret_ref, sources, refs = refs[0], (refs[1:4], refs[4:7]), refs[7:]
    g_ref, u_ref, sg_ref, su_ref, wsi_ref, wsd_ref = refs[:6]
    dy_ref, dg_ref, du_ref, dsg_ref, dsu_ref = refs[6:11]
    part_refs, (gated_ref, acc_ref) = refs[11 : 11 + members], refs[11 + members :]
    step, last = pl.program_id(0), pl.num_programs(0) - 1
    capacity, width = dy_ref.shape
    tokens = grad_refs[0].shape[0]
    tiles = [slice(r, r + tokens) for r in range(0, capacity, tokens)]

    @pl.when(step == 0)
    def _():
        for k in range(members):
            t = slice(k * tokens, (k + 1) * tokens)
            grad = grad_refs[k][...].astype(F32)
            weight = meta_ref[t, SPOT : SPOT + 1]
            gated_ref[k, :, :] = (weight * grad).astype(BF)
            product = grad * ret_ref[t, :].astype(F32)
            high = product.astype(BF)
            low = (product - high.astype(F32)).astype(BF)
            ones = jnp.ones((TAIL, width), BF)
            total = nt(ones, high) + nt(ones, low)
            high = total.astype(BF).astype(F32)
            row = lax.broadcasted_iota(I32, total.shape, 0)
            tail = jnp.where(row == 0, high, jnp.where(row == 1, total - high, 0.0))
            part_refs[k][tokens : tokens + TAIL, :] = jnp.zeros((TAIL, width), BF)
            part_refs[k][tokens : tokens + TAIL, :tokens] = tail.astype(BF)
        for r in tiles:
            dy_ref[r, :] = dispatch(slot_ref, [gated_ref.at[k] for k in range(members)], r.start, tokens)
            acc_ref[r, :] = jnp.zeros((tokens, width), F32)

    def units(wg_ref, wu_ref, wd_ref):
        for r in tiles:
            dg, du = act_grads(g_ref[r, :], u_ref[r, :], nt(dy_ref[r, :], wd_ref[...]))
            dg_ref[r, :], du_ref[r, :] = dg, du
            acc_ref[r, :] += nt(dg, wg_ref[...]) + nt(du, wu_ref[...])

    from_either(which_ref, sources, units)

    @pl.when(step == last)
    def _():
        rows = acc_ref[...].astype(BF)
        quarter = wsd_ref.shape[0]
        for k in range(members):
            t = slice(k * tokens, (k + 1) * tokens)
            dsg, dsu = act_grads(sg_ref[t, :], su_ref[t, :], nt(grad_refs[k][...], wsd_ref[...]))
            dsg_ref[t, :], dsu_ref[t, :] = dsg, dsu
            back = nt(dsg, wsi_ref[:, :quarter]) + nt(dsu, wsi_ref[:, quarter:])
            back = back + nn(slot_columns(info_ref[t, :], capacity), rows)
            part_refs[k][:tokens, :] = back.astype(BF)


def whole_block(*shape):
    return pl.BlockSpec(shape, lambda i, which: (0,) * len(shape), pipeline_mode=pl.Buffered(1))


def expert_specs(width):
    steps = FF // TILE

    def tiles(own):
        def at(i, which):
            return i * (which[1] if own else 1 - which[1])

        return [
            pl.BlockSpec((width, TILE), lambda i, which: (0, at(i, which))),
            pl.BlockSpec((width, TILE), lambda i, which: (0, steps + at(i, which))),
            pl.BlockSpec((TILE, width), lambda i, which: (at(i, which), 0)),
        ]

    return tiles(True) + tiles(False)


def expert_args(experts):
    return [w for w_in, w_down in experts for w in (w_in, w_in, w_down)]


def moe_call(kernel, shapes, in_specs, out_tiled, scratch, args, work):
    whole = [whole_block(*shape) for shape, _ in shapes]
    tiled = pl.BlockSpec((shapes[0][0][0], TILE), lambda i, which: (0, i))
    return pl.pallas_call(
        kernel,
        out_shape=[jax.ShapeDtypeStruct(*shape) for shape in shapes],
        grid_spec=pltpu.PrefetchScalarGridSpec(
            num_scalar_prefetch=1,
            grid=(FF // TILE,),
            in_specs=in_specs,
            out_specs=whole[:1] + [tiled] * out_tiled + whole[1 + out_tiled :],
            scratch_shapes=scratch,
        ),
        compiler_params=pltpu.CompilerParams(vmem_limit_bytes=56 << 20),
        cost_estimate=pl.CostEstimate(flops=work, bytes_accessed=30 << 20, transcendentals=1 << 20),
    )(*args)


def moe_work(width, capacity, everyone, quarter):
    return 2 * width * (capacity * (3 * FF + 2 * everyone) + 3 * everyone * quarter)


def moe_forward(which, slot, info, w_small, blocks, experts, w_sin, w_sdown, capacity, count):
    members, (tokens, width), quarter = len(blocks), blocks[0].shape, w_sdown.shape[0]
    everyone = members * tokens
    shapes = [((capacity, width), BF)] + [((capacity, FF), BF)] * 3
    shapes += [((everyone, 128), F32), ((everyone, width), BF)] + [((everyone, quarter), BF)] * 3
    shapes += [((tokens, width), BF)] * members
    in_specs = [whole_block(members, tokens), whole_block(everyone, 128), whole_block(width, 128)]
    in_specs += [whole_block(tokens, width)] * members + expert_specs(width)
    in_specs += [whole_block(width, 2 * quarter), whole_block(quarter, width)]
    return moe_call(
        functools.partial(moe_forward_kernel, members, count),
        shapes,
        in_specs,
        3,
        [pltpu.VMEM((capacity, width), F32), pltpu.VMEM((capacity, width), BF)],
        (which, slot, info, w_small, *blocks, *expert_args(experts), w_sin, w_sdown),
        moe_work(width, capacity, everyone, quarter),
    )


def moe_backward(which, slot, info, meta, blocks, ret, experts, gate, up, sg, su, w_sin, w_sdown):
    members, (tokens, width), quarter = len(blocks), blocks[0].shape, w_sdown.shape[0]
    everyone, capacity = members * tokens, gate.shape[0]
    shapes = [((capacity, width), BF)] + [((capacity, FF), BF)] * 2
    shapes += [((everyone, quarter), BF)] * 2 + [((tokens + TAIL, width), BF)] * members
    in_specs = [whole_block(members, tokens), whole_block(everyone, 128), whole_block(everyone, 128)]
    in_specs += [whole_block(tokens, width)] * members + [whole_block(everyone, width)] + expert_specs(width)
    in_specs += [pl.BlockSpec((capacity, TILE), lambda i, which: (0, i))] * 2
    in_specs += [whole_block(everyone, quarter)] * 2
    in_specs += [whole_block(width, 2 * quarter), whole_block(quarter, width)]
    return moe_call(
        functools.partial(moe_backward_kernel, members),
        shapes,
        in_specs,
        2,
        [pltpu.VMEM((members, tokens, width), BF), pltpu.VMEM((capacity, width), F32)],
        (which, slot, info, meta, *blocks, ret, *expert_args(experts), gate, up, sg, su, w_sin, w_sdown),
        moe_work(width, capacity, everyone, quarter),
    )


def after(values, *others):
    return lax.optimization_barrier((values, others))[0]


class Weights:
    def __init__(self, core, members, gains, w_qkv, w_out, w_router, *rest):
        self.core, self.members, self.width = core, members, w_out.shape[1]
        self.experts = w_router.shape[1]
        rows, extra = w_qkv.shape[0], self.experts + 2
        small = jnp.concatenate([w_router, gains.T, jnp.zeros((rows, 128 - extra), BF)], axis=1)
        self.first_shares = self.shares(jnp.concatenate([w_qkv, small], axis=1))
        self.out_shares = self.shares(w_out)
        self.w_sin, self.w_sdown, self.w_ein, self.w_edown = rest

    def both(self, mine):
        other = swap_cores(mine)
        return by_core(self.core, mine, other), by_core(self.core, other, mine)

    def shares(self, shard):
        mine, theirs = half_of(shard, self.core), half_of(shard, 1 - self.core)
        other = swap_cores(theirs)
        return by_core(self.core, mine, other), by_core(self.core, other, mine)

    def both_halves(self, full):
        blocks, rows, columns = full.shape
        other = swap_cores(full)
        halves = [by_core(self.core, full, other), by_core(self.core, other, full)]
        return jnp.stack(halves, axis=1).reshape(blocks * 2 * rows, columns)

    def permuted(self, part):
        me, blocks = lax.axis_index(EXP), jnp.stack(gather_blocks(part, self.members))
        return jnp.concatenate(
            [lax.dynamic_slice_in_dim(blocks, me ^ j, 1, 0) for j in range(self.members)]
        )

    def split_first(self, first):
        at = 3 * self.width
        small = first[:, at : at + 128]
        return first[:, :at], small, small[:, self.experts : self.experts + 2].T.astype(F32)

    def shared_in(self, w_sin):
        me, quarter = lax.axis_index(EXP), FF // self.members
        blocks = []
        for k in range(self.members):
            at = (me ^ k) * quarter
            parts = [lax.dynamic_slice_in_dim(w_sin, start + at, quarter, 1) for start in (0, FF)]
            blocks.append(jnp.concatenate(parts, axis=1))
        blocks = jnp.stack(scatter_blocks(blocks))
        return jnp.concatenate([lax.dynamic_index_in_dim(blocks, me ^ j, 0, False) for j in range(self.members)])


def add_low(a, b):
    return (a.astype(F32) + b.astype(F32)).astype(BF)


class LineSums:
    def __init__(self):
        lane = lax.axis_index(DP)
        self.middle = (lane == 1) | (lane == 2)
        self.now, self.waiting, self.flights, self.done = 0, [], [], {}

    def add(self, section, name, chunks):
        self.waiting += [((section, name, i), chunk) for i, chunk in enumerate(chunks)]

    def busy(self):
        return self.waiting or self.flights

    def step(self, main, count=WINDOW_STEP[0], steps=WINDOW_STEP[1]):
        self.now += 1
        landed = [flight for flight in self.flights if flight[0] <= self.now]
        self.flights = [flight for flight in self.flights if flight[0] > self.now]
        fresh, self.waiting = self.waiting[:count], self.waiting[count:]
        tied = (main, [flight[3:] for flight in landed], [item[1] for item in fresh])
        main, states, chunks = lax.optimization_barrier(tied)

        def launch(stage, key, value, axis, pairs, wait):
            got = lax.ppermute(value, axis, pairs)
            self.flights.append((self.now + wait, stage, key, value, got))

        for (_, stage, key, *_), (value, got) in zip(landed, states):
            if stage == 0:
                launch(1, key, add_low(value, got), DP, [(1, 2), (2, 1)], steps)
            elif stage == 1:
                launch(2, key, add_low(value, got), DP, [(1, 0), (2, 3)], steps)
            elif stage == 2:
                pair = (1, 0) if key[0] == 0 else (0, 1)
                launch(3, key, jnp.where(self.middle, value, got), SEC, [pair], 1)
            else:
                self.done[key] = (value, got)
        for (key, _), chunk in zip(fresh, chunks):
            launch(0, key, chunk, DP, [(0, 1), (3, 2)], steps)
        return main

    def result(self, section, name):
        keys = sorted(key for key in self.done if key[:2] == (section, name))
        return [self.done[key] for key in keys]


def cut(v, count):
    rows = v.shape[0] // count
    return [v[i * rows : (i + 1) * rows] for i in range(count)]


def to_heads(v, lanes, parts):
    tokens, columns = v.shape
    per = columns // (parts * lanes)
    split = v.reshape(tokens, parts, lanes, per).transpose(2, 0, 1, 3).reshape(lanes, tokens, parts * per)
    return a2a(split, DP).reshape(lanes * tokens, parts * per)


def to_tokens(v, lanes, parts):
    pack, columns = v.shape
    tokens, per = pack // lanes, columns // parts
    got = a2a(v.reshape(lanes, tokens, columns), DP).reshape(lanes, tokens, parts, per)
    return got.transpose(1, 2, 0, 3).reshape(tokens, lanes * columns)


def add_blocks(first, blocks):
    return functools.reduce(jnp.add, [block.astype(F32) for block in blocks], first)


def layer_mlp(middle, context, weights, beside=None):
    gain, w_small, w_sin, w_sdown, experts, which = weights
    me, slot, info, capacity, count = context
    members = slot.shape[0]
    hidden, scale = norm_apply(middle, gain)
    blocks = gather_blocks(hidden, members)
    out = moe_forward(which, slot, info, w_small, blocks, experts, w_sin, w_sdown, capacity, count)
    if beside is not None:
        out = beside(out)
    parts = scatter_blocks(out[9:])
    return add_blocks(middle, parts), (scale, hidden, blocks, *out[:9])


def mlp_backward(grad_blocks, middle, saved, context, weights, sums, ready, kernel_done):
    gain, w_small, w_sin, w_sdown, expert_weights, which = weights
    me, slot, info, capacity, experts = context
    scale, hidden, blocks, rows, gate, up, act, meta, ret, sg, su, sact = saved
    members, (tokens, width) = len(blocks), middle.shape
    out = moe_backward(
        which, slot, info, meta, grad_blocks, ret, expert_weights, gate, up, sg, su, w_sin, w_sdown
    )
    out = sums.step(kernel_done(out))
    dy, dg, du, dsg, dsu = out[:5]
    parts = scatter_blocks(out[5:])
    ready((rows, act, dy, dg, du), (blocks, sact, grad_blocks, dsg, dsu))
    parts = sums.step(parts)
    dh2 = add_blocks(jnp.zeros(middle.shape, F32), [part[:tokens] for part in parts])
    tails = [part[tokens : tokens + 2, :tokens].astype(F32) for part in parts]
    column = jnp.arange(experts, dtype=I32)[None, :]
    dgates = sum(
        jnp.where(column == (me ^ k), (tail[0] + tail[1])[:, None], 0.0) for k, tail in enumerate(tails)
    )
    router, chosen = meta[:tokens, :experts], info[:tokens, :experts]
    picked = jnp.sum(router * chosen, axis=-1, keepdims=True)
    inner = jnp.sum(dgates * router * chosen, axis=-1, keepdims=True) / picked
    dprob = chosen * (dgates - inner) / picked
    dlogits = (router * (dprob - jnp.sum(router * dprob, axis=-1, keepdims=True))).astype(BF)
    dh2 = dh2 + mm(dlogits, w_small[:, :experts], 1, 1)
    dmiddle_norm, dgain = norm_backward(dh2, middle, scale, gain)
    dmiddle = grad_blocks[0].astype(F32) + dmiddle_norm
    return dmiddle, dgain, dlogits


def halves(rows_of, grads, core):
    send = mm(half_of(rows_of, 1 - core, 1), grads, 0, 0, out=BF)
    keep = mm(half_of(rows_of, core, 1), grads, 0, 0)
    return (keep + swap_cores(send).astype(F32)).astype(BF)


def halves_by_member(rows_of, grads, core, members):
    split = rows_of.reshape(rows_of.shape[0], members, 2, -1)

    def side(which):
        return lax.dynamic_index_in_dim(split, which, 2, False).reshape(rows_of.shape[0], -1)

    send = mm(side(1 - core), grads, 0, 0, out=BF)
    keep = mm(side(core), grads, 0, 0)
    return (keep + swap_cores(send).astype(F32)).astype(BF).reshape(members, -1, grads.shape[1])


def expert_grads(terms, core):
    rows, act, dy, dg, du = terms
    g_in = jnp.concatenate([halves(rows, dg, core), halves(rows, du, core)], axis=1)
    return halves(act, dy, core), g_in


def shared_grads(terms, core):
    blocks, sact, grad_blocks, dsg, dsu = terms
    members = len(blocks)
    hidden_all, grad_all = jnp.concatenate(blocks), jnp.concatenate(grad_blocks)
    g_in = halves_by_member(hidden_all, jnp.concatenate([dsg, dsu], axis=1), core, members)
    return halves(sact, grad_all, core), a2a(g_in, EXP)


def dense_grads(terms, core, members):
    hidden_one, dqkv, mixed, dattn, hidden_two, dlogits, dgains = terms
    width, experts = hidden_one.shape[1], dlogits.shape[1]
    small = jnp.concatenate(
        [mm(hidden_two, dlogits, 0, 0), jnp.stack(dgains, axis=1), jnp.zeros((width, 126 - experts), F32)],
        axis=1,
    )
    split = small.reshape(members, 2, -1, 128)
    send = lax.dynamic_index_in_dim(split, 1 - core, 1, False).astype(BF)
    keep = lax.dynamic_index_in_dim(split, core, 1, False)
    small = (keep + swap_cores(send).astype(F32)).astype(BF)
    g_out = halves_by_member(mixed, dattn, core, members)
    g_qkv = halves_by_member(hidden_one, dqkv, core, members)
    return jnp.concatenate([g_qkv, g_out, small], axis=2)


def member_sum(parts):
    return jnp.sum(parts.astype(F32), axis=0).astype(BF)


def local(
    inputs, cotangent, lengths, deal, routes, order, gains, w_qkv, w_out, w_router, w_shared_in, w_shared_down,
    w_expert_in, w_expert_down,
):
    core, me = lax.axis_index(SEC), lax.axis_index(EXP)
    members, lanes = lax.axis_size(EXP), lax.axis_size(DP)
    batches, _, tokens, width = inputs.shape
    experts = w_router.shape[2]
    assert batches == lax.axis_size(SEC) == 2 and w_expert_in.shape[1] == 1 and experts == members
    w = Weights(
        core, members, gains[0], w_qkv[0], w_out[0], w_router[0], w_shared_in[0], w_shared_down[0],
        w_expert_in[0, 0], w_expert_down[0, 0],
    )
    first_low = lax.dynamic_index_in_dim(inputs[:, 0], core, 0, False)
    grad_low = lax.dynamic_index_in_dim(cotangent[:, 0], core, 0, False)
    row = lax.dynamic_index_in_dim(deal, core * members + me, 0, False)
    ends = jnp.cumsum(lax.dynamic_index_in_dim(lengths, row, 0, False))[:-1].astype(I32)
    qkv_0, w_small_0, gains_0 = w.split_first(w.both_halves(w.permuted(w.first_shares[0])))
    current_0 = first_low.astype(F32)
    hidden_0, scale_0 = norm_apply(current_0, gains_0[0])
    projected = mm(hidden_0, qkv_0, out=BF)
    pairs = lax.dynamic_index_in_dim(routes[:, 0], core, 0, False).reshape(-1)
    places = lax.dynamic_index_in_dim(order[:, 0], core, 0, False)
    same = pairs[:, None] == pairs[None, :]
    rank = jnp.sum((same & (places[None, :] < places[:, None])).astype(I32), axis=1)
    code = jnp.stack(gather_blocks(after(pairs * (2 * tokens) + rank, projected), members))
    owner = me ^ jnp.arange(members, dtype=I32)
    pairs_all, rank_all = code // (2 * tokens), code % (2 * tokens)
    onehot = (pairs_all[:, :, None] == jnp.arange(experts, dtype=I32)).astype(I32)
    counts = jnp.sum(onehot, axis=1)
    lower = (owner[None, :] < owner[:, None]).astype(I32)
    before = jnp.sum(lower[:, :, None] * counts[None], axis=1)
    place = jnp.sum(onehot * before[:, None, :], axis=2) + rank_all
    capacity = 2 * tokens * members // experts
    slot = jnp.where((pairs_all == me) & (place < capacity), place, -1)
    slot = jnp.max(slot.reshape(members, tokens, 2), axis=2)
    column = jnp.arange(128, dtype=I32)[None, :]
    named = pairs_all.reshape(members * tokens, 2)
    chosen = (named[:, :1] == column) | (named[:, 1:] == column)
    info = jnp.where(column == SPOT, slot.reshape(-1, 1).astype(F32), chosen.astype(F32))

    w_out_0 = w.both_halves(w.permuted(after(w.out_shares[0], projected)))
    shared_in = w.shared_in(after(w.w_sin, projected))
    shared = (shared_in, w.w_sdown)
    shared = (shared, (swap_cores(shared_in), swap_cores(w.w_sdown)))
    expert_weights = ((w.w_ein, w.w_edown), (swap_cores(w.w_ein), swap_cores(w.w_edown)))
    which = [jnp.stack([me, (core == s).astype(I32)]) for s in range(2)]
    heads_0 = to_heads(projected, lanes, 3)
    heads_0, slot, info, w_out_0 = lax.optimization_barrier((heads_0, slot, info, w_out_0))
    context = (me, slot, info, capacity, experts)
    later = jnp.concatenate([w.first_shares[1], w.out_shares[1]], axis=1)
    mixed_0, shared = lax.optimization_barrier((attention_forward(ends, heads_0, tokens), shared))
    mixed_0 = to_tokens(mixed_0, lanes, 1)
    shared_first = [by_core(core, mine, other) for mine, other in zip(*shared)]
    mixed_0, shared_first = lax.optimization_barrier((mixed_0, shared_first))
    shared_second = [by_core(core, other, mine) for mine, other in zip(*shared)]
    middle_0 = current_0 + mm(mixed_0, w_out_0)
    gathered = []

    def land(out):
        out, full = lax.optimization_barrier((out, lax.all_gather(after(later, heads_0), EXP)))
        gathered.append(full)
        return out

    mlp_0 = (gains_0[1], w_small_0, *shared_first, expert_weights, which[0])
    out_0, saved_0 = layer_mlp(middle_0, context, mlp_0, land)
    dense_1 = w.both_halves(gathered[0])
    low_0, dense_1, shared_second = lax.optimization_barrier((out_0.astype(BF), dense_1, shared_second))
    qkv_1, w_small_1, gains_1 = w.split_first(dense_1)
    w_out_1 = dense_1[:, 3 * width + 128 :]
    current_1 = low_0.astype(F32)
    hidden_1, scale_1 = norm_apply(current_1, gains_1[0])
    projected = mm(hidden_1, qkv_1, out=BF)
    grad_blocks = gather_blocks(after(grad_low, projected), members)
    heads_1 = to_heads(projected, lanes, 3)
    heads_1, grad_blocks = lax.optimization_barrier((heads_1, grad_blocks))
    mixed_1 = to_tokens(attention_forward(ends, heads_1, tokens), lanes, 1)
    middle_1 = current_1 + mm(mixed_1, w_out_1)
    mlp_1 = (gains_1[1], w_small_1, *shared_second, expert_weights, which[1])
    out_1, saved_1 = layer_mlp(middle_1, context, mlp_1)
    low_1 = out_1.astype(BF)

    sums = LineSums()

    def backward(section, grad_blocks, current, hidden, scale, heads, mixed, middle, saved, gain, w_qkv_s, w_out_s, mlp, beside=None):
        shared = []

        def kernel_done(out):
            if beside is None:
                return out
            out, parts = lax.optimization_barrier((out, a2a(beside, EXP)))
            sums.add(1 - section, 4, [member_sum(parts)])
            return out

        def ready(terms, shared_terms):
            down, ein = expert_grads(terms, core)
            sums.add(section, 0, cut(down, CHUNKS[0]))
            sums.add(section, 1, cut(ein, CHUNKS[1]))
            shared.append(shared_terms)

        dmiddle, dgain_two, dlogits = mlp_backward(
            grad_blocks, middle, saved, context, mlp, sums, ready, kernel_done
        )
        dattn = dmiddle.astype(BF)
        dheads = to_heads(mm(dattn, w_out_s, 1, 1, out=BF), lanes, 1)
        g_sdown, g_sin = shared_grads(shared[0], core)
        sums.add(section, 2, [g_sdown])
        sums.add(section, 3, [g_sin.reshape(-1, g_sin.shape[2])])
        dheads = sums.step(dheads)
        dheads = sums.step(attention_backward(ends, heads, dheads, tokens))
        dqkv = sums.step(to_tokens(dheads, lanes, 3))
        dinput, dgain_one = norm_backward(mm(dqkv, w_qkv_s, 1, 1), current, scale, gain)
        dense = (hidden, dqkv, mixed, dattn, saved[1], dlogits, (dgain_one, dgain_two))
        return dmiddle + dinput, dense_grads(dense, core, members)

    grad_1, dense_1 = backward(
        1, grad_blocks, current_1, hidden_1, scale_1, heads_1, mixed_1, middle_1, saved_1, gains_1[0], qkv_1,
        w_out_1, mlp_1,
    )
    grad_blocks, dense_1 = lax.optimization_barrier((gather_blocks(grad_1.astype(BF), members), dense_1))
    grad_blocks = sums.step(grad_blocks)
    grad_0, dense_0 = backward(
        0, grad_blocks, current_0, hidden_0, scale_0, heads_0, mixed_0, middle_0, saved_0, gains_0[0], qkv_0,
        w_out_0, mlp_0, dense_1,
    )
    sums.add(0, 4, [member_sum(a2a(dense_0, EXP))])
    quarter = FF // members

    def by_columns(half):
        blocks = half.reshape(members, -1, 2 * quarter)
        return jnp.concatenate(
            [blocks[j][:, at : at + quarter] for at in (0, quarter) for j in range(members)], axis=1
        )

    def whole(name):
        own_0, got_0 = zip(*sums.result(0, name))
        own_1, got_1 = zip(*sums.result(1, name))
        pairs = zip(own_0 + got_0, got_1 + own_1)
        parts = [by_core(core, a, b) for a, b in pairs]
        return jnp.concatenate([by_columns(v) if name == 3 else v for v in parts]).astype(F32)

    def complete(name):
        return all(len(sums.result(section, name)) == CHUNKS[name] for section in range(2))

    results = {}
    while sums.busy():
        results = sums.step(results, *TAIL_STEP)
        results.update({name: whole(name) for name in range(5) if name not in results and complete(name)})

    def to_section(of_0, of_1):
        mine = by_core(core, of_0, of_1)
        other = swap_cores(by_core(core, of_1, of_0))
        both = jnp.stack([by_core(core, mine, other), by_core(core, other, mine)])
        return both[None, :, None]

    down, ein, sdown, sin, dense = [results[name] for name in range(5)]
    at = 4 * width
    return (
        to_section(low_0, low_1),
        to_section(grad_0, grad_1),
        dense[:, at + experts : at + experts + 2].T[None],
        dense[None, :, : 3 * width],
        dense[None, :, 3 * width : at],
        dense[None, :, at : at + experts],
        sin[None],
        sdown[None],
        ein[None, None],
        down[None, None],
    )


def solution(mesh):
    tokens = P(None, EXP, DP, None)
    dense = P(SEC, EXP, None)
    expert = P(SEC, EXP, None, None)
    both = P(SEC, None, EXP, DP, None)
    gains = P(SEC, None, EXP)
    return jax.shard_map(
        local,
        mesh=mesh,
        in_specs=(tokens, tokens, P(), P(), tokens, P(None, EXP, DP), gains)
        + (dense,) * 5
        + (expert,) * 2,
        out_specs=(both, both, gains) + (dense,) * 5 + (expert,) * 2,
        check_vma=False,
    )
```

```python
import functools
import jax
import jax.numpy as jnp
from jax import lax
from jax.experimental import pallas as pl
from jax.experimental.pallas import tpu as pltpu
from jax.sharding import PartitionSpec as P

HEADS = 12
HEAD = 64
FF = 2048
EPS = 1e-06

SEC, DP, EXP = "section", "dp", "expert"
BF, F32, I32 = jnp.bfloat16, jnp.float32, jnp.int32
SWAP = [(0, 1), (1, 0)]


def mm(a, b, ca=1, cb=0, out=F32):
    r = lax.dot_general(a, b, (((ca,), (cb,)), ((), ())), preferred_element_type=F32)
    return r.astype(out)


def swap_cores(v):
    return lax.ppermute(v, SEC, SWAP)


def a2a(v, axis):
    return lax.all_to_all(v, axis, split_axis=0, concat_axis=0, tiled=True)


def gather(v, axis):
    return lax.all_gather(v, axis, axis=0, tiled=True)


def xor_pairs(count, k):
    return [(i, i ^ k) for i in range(count)]


def gather_blocks(v, members):
    return [v] + [lax.ppermute(v, EXP, xor_pairs(members, k)) for k in range(1, members)]


def scatter_blocks(blocks):
    count = len(blocks)
    return [blocks[0]] + [lax.ppermute(blocks[k], EXP, xor_pairs(count, k)) for k in range(1, count)]


def half_of(v, which, axis=0):
    size = v.shape[axis] // 2
    return lax.dynamic_slice_in_dim(v, which * size, size, axis)


def by_core(core, first, second):
    return jnp.where(core == 0, first, second)


def norm_apply(values, gain):
    scale = lax.rsqrt(jnp.mean(values * values, axis=-1, keepdims=True) + EPS)
    return (values * scale * gain).astype(BF), scale


def norm_backward(grad_hidden, values, scale, gain):
    normed = values * scale
    grad_gain = jnp.sum(grad_hidden * normed, axis=0)
    grad_normed = grad_hidden * gain
    grad_values = scale * (
        grad_normed - normed * jnp.mean(grad_normed * normed, axis=-1, keepdims=True)
    )
    return grad_values, grad_gain


def silu(v):
    return v * jax.nn.sigmoid(v)


def silu_parts(v):
    logistic = jax.nn.sigmoid(v)
    return v * logistic, logistic * (1.0 + v * (1.0 - logistic))


def block_mask(ends_ref, first_row, rows, cols):
    q = first_row + lax.broadcasted_iota(I32, (rows, cols), 0)
    k = lax.broadcasted_iota(I32, (rows, cols), 1)
    start = jnp.zeros((rows, cols), I32)
    for i in range(ends_ref.shape[0]):
        end = ends_ref[i]
        start = jnp.where(q >= end, end, start)
    return (k <= q) & (k >= start)


def head_slices(ref, rows, head, per, parts):
    return [ref[rows, (part * per + head) * HEAD : (part * per + head + 1) * HEAD] for part in parts]


def block_probs(q, k, mask):
    scores = lax.dot_general(q, k, (((1,), (1,)), ((), ())), preferred_element_type=F32)
    scores = jnp.where(mask, scores * (HEAD**-0.5), -1e30)
    raised = jnp.exp(scores - jnp.max(scores, axis=-1, keepdims=True))
    return raised / jnp.sum(raised, axis=-1, keepdims=True)


def attention_forward_kernel(block, per, ends_ref, qkv_ref, out_ref):
    pack = qkv_ref.shape[0]
    for i in range(pack // block):
        rows, reach = slice(i * block, (i + 1) * block), slice(0, (i + 1) * block)
        mask = block_mask(ends_ref, i * block, block, (i + 1) * block)
        for head in range(per):
            (q,) = head_slices(qkv_ref, rows, head, per, (0,))
            k, v = head_slices(qkv_ref, reach, head, per, (1, 2))
            probs = block_probs(q, k, mask).astype(BF)
            mixed = jnp.dot(probs, v, preferred_element_type=F32)
            out_ref[rows, head * HEAD : (head + 1) * HEAD] = mixed.astype(BF)


def attention_backward_kernel(block, per, ends_ref, qkv_ref, grad_ref, out_ref, dk_ref, dv_ref):
    pack = qkv_ref.shape[0]
    dk_ref[...] = jnp.zeros_like(dk_ref)
    dv_ref[...] = jnp.zeros_like(dv_ref)
    for i in range(pack // block):
        rows, reach = slice(i * block, (i + 1) * block), slice(0, (i + 1) * block)
        mask = block_mask(ends_ref, i * block, block, (i + 1) * block)
        for head in range(per):
            (q,) = head_slices(qkv_ref, rows, head, per, (0,))
            k, v = head_slices(qkv_ref, reach, head, per, (1, 2))
            grad = grad_ref[rows, head * HEAD : (head + 1) * HEAD]
            probs = block_probs(q, k, mask)
            dprobs = lax.dot_general(grad, v, (((1,), (1,)), ((), ())), preferred_element_type=F32)
            delta = jnp.sum(probs * dprobs, axis=-1, keepdims=True)
            dscores = (probs * (dprobs - delta)).astype(BF)
            dq = jnp.dot(dscores, k, preferred_element_type=F32) * (HEAD**-0.5)
            out_ref[rows, head * HEAD : (head + 1) * HEAD] = dq.astype(BF)
            over_queries = (((0,), (0,)), ((), ()))
            dk_ref[head, reach, :] += lax.dot_general(
                dscores, q, over_queries, preferred_element_type=F32
            )
            dv_ref[head, reach, :] += lax.dot_general(
                probs.astype(BF), grad, over_queries, preferred_element_type=F32
            )
    for head in range(per):
        at = (per + head) * HEAD
        out_ref[:, at : at + HEAD] = (dk_ref[head] * (HEAD**-0.5)).astype(BF)
        at = (2 * per + head) * HEAD
        out_ref[:, at : at + HEAD] = dv_ref[head].astype(BF)


def vmem():
    return pl.BlockSpec(memory_space=pltpu.VMEM)


def attention_forward(ends, qkv, block):
    pack, columns = qkv.shape
    per = columns // (3 * HEAD)
    return pl.pallas_call(
        functools.partial(attention_forward_kernel, block, per),
        out_shape=jax.ShapeDtypeStruct((pack, per * HEAD), BF),
        in_specs=[pl.BlockSpec(memory_space=pltpu.SMEM), vmem()],
        out_specs=vmem(),
        compiler_params=pltpu.CompilerParams(vmem_limit_bytes=16 << 20),
        cost_estimate=pl.CostEstimate(
            flops=4 * per * pack * pack * HEAD, bytes_accessed=8 * pack * columns // 3, transcendentals=per * pack * pack
        ),
    )(ends, qkv)


def attention_backward(ends, qkv, grad, block):
    pack, columns = qkv.shape
    per = columns // (3 * HEAD)
    return pl.pallas_call(
        functools.partial(attention_backward_kernel, block, per),
        out_shape=jax.ShapeDtypeStruct((pack, columns), BF),
        in_specs=[pl.BlockSpec(memory_space=pltpu.SMEM), vmem(), vmem()],
        out_specs=vmem(),
        scratch_shapes=[pltpu.VMEM((per, pack, HEAD), F32)] * 2,
        compiler_params=pltpu.CompilerParams(vmem_limit_bytes=16 << 20),
        cost_estimate=pl.CostEstimate(
            flops=10 * per * pack * pack * HEAD, bytes_accessed=16 * pack * columns // 3, transcendentals=per * pack * pack
        ),
    )(ends, qkv, grad)


SPOT = 64
TAIL = 16
TILE = 512
WINDOW_STEP = (1, 2)
TAIL_STEP = (1, 2)
CHUNKS = (1, 2, 1, 1, 1)


def nt(a, b):
    return lax.dot_general(a, b, (((1,), (1,)), ((), ())), preferred_element_type=F32)


def nn(a, b):
    return jnp.dot(a, b, preferred_element_type=F32)


def slot_rows(slot_ref, k, first, count):
    row = slot_ref[k : k + 1, :]
    place = first + lax.broadcasted_iota(I32, (count, row.shape[1]), 0)
    return (place == row).astype(F32).astype(BF)


def slot_columns(info, capacity):
    column = info[:, SPOT : SPOT + 1]
    place = lax.broadcasted_iota(I32, (info.shape[0], capacity), 1).astype(F32)
    return (place == column).astype(F32).astype(BF)


def dispatch(slot_ref, block_refs, first, count):
    total = None
    for k, ref in enumerate(block_refs):
        part = nn(slot_rows(slot_ref, k, first, count), ref[...])
        total = part if total is None else total + part
    return total.astype(BF)


def from_either(which_ref, sources, body):
    @pl.when(which_ref[1] == 1)
    def _():
        body(*sources[0])

    @pl.when(which_ref[1] == 0)
    def _():
        body(*sources[1])


def moe_forward_kernel(members, experts, *refs):
    which_ref, slot_ref, info_ref, router_ref = refs[:4]
    h_refs, refs = refs[4 : 4 + members], refs[4 + members :]
    sources, (wsi_ref, wsd_ref), refs = (refs[:3], refs[3:6]), refs[6:8], refs[3:]
    rows_ref, g_ref, u_ref, a_ref, meta_ref, ret_ref, sg_ref, su_ref, sa_ref = refs[5:14]
    part_refs, (acc_ref, y_ref) = refs[14 : 14 + members], refs[14 + members :]
    step, last = pl.program_id(0), pl.num_programs(0) - 1
    capacity, tokens = rows_ref.shape[0], h_refs[0].shape[0]
    tiles = [slice(r, r + tokens) for r in range(0, capacity, tokens)]

    @pl.when(step == 0)
    def _():
        for r in tiles:
            rows_ref[r, :] = dispatch(slot_ref, h_refs, r.start, tokens)
            acc_ref[r, :] = jnp.zeros((tokens, acc_ref.shape[1]), F32)

    def units(wg_ref, wu_ref, wd_ref):
        for r in tiles:
            x = rows_ref[r, :]
            gate, up = nn(x, wg_ref[...]), nn(x, wu_ref[...])
            act = (gate * jax.nn.sigmoid(gate) * up).astype(BF)
            g_ref[r, :], u_ref[r, :], a_ref[r, :] = gate.astype(BF), up.astype(BF), act
            acc_ref[r, :] += nn(act, wd_ref[...])

    from_either(which_ref, sources, units)

    @pl.when(step == last)
    def _():
        for r in tiles:
            y_ref[r, :] = acc_ref[r, :].astype(BF)
        quarter = wsd_ref.shape[0]
        for k in range(members):
            t = slice(k * tokens, (k + 1) * tokens)
            h, info = h_refs[k][...], info_ref[t, :]
            lane = lax.broadcasted_iota(I32, info.shape, 1)
            logits = jnp.where(lane < experts, nn(h, router_ref[...]), -1e30)
            raised = jnp.exp(logits - jnp.max(logits, axis=-1, keepdims=True))
            probs = raised / jnp.sum(raised, axis=-1, keepdims=True)
            chosen = jnp.where(lane < experts, info, 0.0)
            picked = jnp.sum(probs * chosen, axis=-1, keepdims=True)
            here = jnp.sum(jnp.where(lane == which_ref[0], probs, 0.0), axis=-1, keepdims=True)
            weight = here / picked
            meta_ref[t, :] = jnp.where(lane == SPOT, weight, probs)
            gate, up = nn(h, wsi_ref[:, :quarter]), nn(h, wsi_ref[:, quarter:])
            act = (gate * jax.nn.sigmoid(gate) * up).astype(BF)
            sg_ref[t, :], su_ref[t, :], sa_ref[t, :] = gate.astype(BF), up.astype(BF), act
            back = nn(slot_columns(info, capacity), y_ref[...])
            ret_ref[t, :] = back.astype(BF)
            part_refs[k][...] = (weight * back + nn(act, wsd_ref[...])).astype(BF)


def act_grads(gate_low, up_low, grad_act):
    gate, up = gate_low.astype(F32), up_low.astype(F32)
    value, slope = silu_parts(gate)
    return (grad_act * up * slope).astype(BF), (grad_act * value).astype(BF)


def moe_backward_kernel(members, *refs):
    which_ref, slot_ref, info_ref, meta_ref = refs[:4]
    grad_refs, refs = refs[4 : 4 + members], refs[4 + members :]
    ret_ref, sources, refs = refs[0], (refs[1:4], refs[4:7]), refs[7:]
    g_ref, u_ref, sg_ref, su_ref, wsi_ref, wsd_ref = refs[:6]
    dy_ref, dg_ref, du_ref, dsg_ref, dsu_ref = refs[6:11]
    part_refs, (gated_ref, acc_ref) = refs[11 : 11 + members], refs[11 + members :]
    step, last = pl.program_id(0), pl.num_programs(0) - 1
    capacity, width = dy_ref.shape
    tokens = grad_refs[0].shape[0]
    tiles = [slice(r, r + tokens) for r in range(0, capacity, tokens)]

    @pl.when(step == 0)
    def _():
        for k in range(members):
            t = slice(k * tokens, (k + 1) * tokens)
            grad = grad_refs[k][...].astype(F32)
            weight = meta_ref[t, SPOT : SPOT + 1]
            gated_ref[k, :, :] = (weight * grad).astype(BF)
            product = grad * ret_ref[t, :].astype(F32)
            high = product.astype(BF)
            low = (product - high.astype(F32)).astype(BF)
            ones = jnp.ones((TAIL, width), BF)
            total = nt(ones, high) + nt(ones, low)
            high = total.astype(BF).astype(F32)
            row = lax.broadcasted_iota(I32, total.shape, 0)
            tail = jnp.where(row == 0, high, jnp.where(row == 1, total - high, 0.0))
            part_refs[k][tokens : tokens + TAIL, :] = jnp.zeros((TAIL, width), BF)
            part_refs[k][tokens : tokens + TAIL, :tokens] = tail.astype(BF)
        for r in tiles:
            dy_ref[r, :] = dispatch(slot_ref, [gated_ref.at[k] for k in range(members)], r.start, tokens)
            acc_ref[r, :] = jnp.zeros((tokens, width), F32)

    def units(wg_ref, wu_ref, wd_ref):
        for r in tiles:
            dg, du = act_grads(g_ref[r, :], u_ref[r, :], nt(dy_ref[r, :], wd_ref[...]))
            dg_ref[r, :], du_ref[r, :] = dg, du
            acc_ref[r, :] += nt(dg, wg_ref[...]) + nt(du, wu_ref[...])

    from_either(which_ref, sources, units)

    @pl.when(step == last)
    def _():
        rows = acc_ref[...].astype(BF)
        quarter = wsd_ref.shape[0]
        for k in range(members):
            t = slice(k * tokens, (k + 1) * tokens)
            dsg, dsu = act_grads(sg_ref[t, :], su_ref[t, :], nt(grad_refs[k][...], wsd_ref[...]))
            dsg_ref[t, :], dsu_ref[t, :] = dsg, dsu
            back = nt(dsg, wsi_ref[:, :quarter]) + nt(dsu, wsi_ref[:, quarter:])
            back = back + nn(slot_columns(info_ref[t, :], capacity), rows)
            part_refs[k][:tokens, :] = back.astype(BF)


def whole_block(*shape):
    return pl.BlockSpec(shape, lambda i, which: (0,) * len(shape), pipeline_mode=pl.Buffered(1))


def expert_specs(width):
    steps = FF // TILE

    def tiles(own):
        def at(i, which):
            return i * (which[1] if own else 1 - which[1])

        return [
            pl.BlockSpec((width, TILE), lambda i, which: (0, at(i, which))),
            pl.BlockSpec((width, TILE), lambda i, which: (0, steps + at(i, which))),
            pl.BlockSpec((TILE, width), lambda i, which: (at(i, which), 0)),
        ]

    return tiles(True) + tiles(False)


def expert_args(experts):
    return [w for w_in, w_down in experts for w in (w_in, w_in, w_down)]


def moe_call(kernel, shapes, in_specs, out_tiled, scratch, args, work):
    whole = [whole_block(*shape) for shape, _ in shapes]
    tiled = pl.BlockSpec((shapes[0][0][0], TILE), lambda i, which: (0, i))
    return pl.pallas_call(
        kernel,
        out_shape=[jax.ShapeDtypeStruct(*shape) for shape in shapes],
        grid_spec=pltpu.PrefetchScalarGridSpec(
            num_scalar_prefetch=1,
            grid=(FF // TILE,),
            in_specs=in_specs,
            out_specs=whole[:1] + [tiled] * out_tiled + whole[1 + out_tiled :],
            scratch_shapes=scratch,
        ),
        compiler_params=pltpu.CompilerParams(vmem_limit_bytes=56 << 20),
        cost_estimate=pl.CostEstimate(flops=work, bytes_accessed=30 << 20, transcendentals=1 << 20),
    )(*args)


def moe_work(width, capacity, everyone, quarter):
    return 2 * width * (capacity * (3 * FF + 2 * everyone) + 3 * everyone * quarter)


def moe_forward(which, slot, info, w_small, blocks, experts, w_sin, w_sdown, capacity, count):
    members, (tokens, width), quarter = len(blocks), blocks[0].shape, w_sdown.shape[0]
    everyone = members * tokens
    shapes = [((capacity, width), BF)] + [((capacity, FF), BF)] * 3
    shapes += [((everyone, 128), F32), ((everyone, width), BF)] + [((everyone, quarter), BF)] * 3
    shapes += [((tokens, width), BF)] * members
    in_specs = [whole_block(members, tokens), whole_block(everyone, 128), whole_block(width, 128)]
    in_specs += [whole_block(tokens, width)] * members + expert_specs(width)
    in_specs += [whole_block(width, 2 * quarter), whole_block(quarter, width)]
    return moe_call(
        functools.partial(moe_forward_kernel, members, count),
        shapes,
        in_specs,
        3,
        [pltpu.VMEM((capacity, width), F32), pltpu.VMEM((capacity, width), BF)],
        (which, slot, info, w_small, *blocks, *expert_args(experts), w_sin, w_sdown),
        moe_work(width, capacity, everyone, quarter),
    )


def moe_backward(which, slot, info, meta, blocks, ret, experts, gate, up, sg, su, w_sin, w_sdown):
    members, (tokens, width), quarter = len(blocks), blocks[0].shape, w_sdown.shape[0]
    everyone, capacity = members * tokens, gate.shape[0]
    shapes = [((capacity, width), BF)] + [((capacity, FF), BF)] * 2
    shapes += [((everyone, quarter), BF)] * 2 + [((tokens + TAIL, width), BF)] * members
    in_specs = [whole_block(members, tokens), whole_block(everyone, 128), whole_block(everyone, 128)]
    in_specs += [whole_block(tokens, width)] * members + [whole_block(everyone, width)] + expert_specs(width)
    in_specs += [pl.BlockSpec((capacity, TILE), lambda i, which: (0, i))] * 2
    in_specs += [whole_block(everyone, quarter)] * 2
    in_specs += [whole_block(width, 2 * quarter), whole_block(quarter, width)]
    return moe_call(
        functools.partial(moe_backward_kernel, members),
        shapes,
        in_specs,
        2,
        [pltpu.VMEM((members, tokens, width), BF), pltpu.VMEM((capacity, width), F32)],
        (which, slot, info, meta, *blocks, ret, *expert_args(experts), gate, up, sg, su, w_sin, w_sdown),
        moe_work(width, capacity, everyone, quarter),
    )


def after(values, *others):
    return lax.optimization_barrier((values, others))[0]


class Weights:
    def __init__(self, core, members, gains, w_qkv, w_out, w_router, *rest):
        self.core, self.members, self.width = core, members, w_out.shape[1]
        self.experts = w_router.shape[1]
        rows, extra = w_qkv.shape[0], self.experts + 2
        small = jnp.concatenate([w_router, gains.T, jnp.zeros((rows, 128 - extra), BF)], axis=1)
        self.first_shares = self.shares(jnp.concatenate([w_qkv, small], axis=1))
        self.out_shares = self.shares(w_out)
        self.w_sin, self.w_sdown, self.w_ein, self.w_edown = rest

    def both(self, mine):
        other = swap_cores(mine)
        return by_core(self.core, mine, other), by_core(self.core, other, mine)

    def shares(self, shard):
        mine, theirs = half_of(shard, self.core), half_of(shard, 1 - self.core)
        other = swap_cores(theirs)
        return by_core(self.core, mine, other), by_core(self.core, other, mine)

    def both_halves(self, full):
        blocks, rows, columns = full.shape
        other = swap_cores(full)
        halves = [by_core(self.core, full, other), by_core(self.core, other, full)]
        return jnp.stack(halves, axis=1).reshape(blocks * 2 * rows, columns)

    def permuted(self, part):
        me, blocks = lax.axis_index(EXP), jnp.stack(gather_blocks(part, self.members))
        return jnp.concatenate(
            [lax.dynamic_slice_in_dim(blocks, me ^ j, 1, 0) for j in range(self.members)]
        )

    def split_first(self, first):
        at = 3 * self.width
        small = first[:, at : at + 128]
        return first[:, :at], small, small[:, self.experts : self.experts + 2].T.astype(F32)

    def shared_in(self, w_sin):
        me, quarter = lax.axis_index(EXP), FF // self.members
        blocks = []
        for k in range(self.members):
            at = (me ^ k) * quarter
            parts = [lax.dynamic_slice_in_dim(w_sin, start + at, quarter, 1) for start in (0, FF)]
            blocks.append(jnp.concatenate(parts, axis=1))
        blocks = jnp.stack(scatter_blocks(blocks))
        return jnp.concatenate([lax.dynamic_index_in_dim(blocks, me ^ j, 0, False) for j in range(self.members)])


def add_low(a, b):
    return (a.astype(F32) + b.astype(F32)).astype(BF)


class LineSums:
    def __init__(self):
        lane = lax.axis_index(DP)
        self.middle = (lane == 1) | (lane == 2)
        self.now, self.waiting, self.flights, self.done = 0, [], [], {}

    def add(self, section, name, chunks):
        self.waiting += [((section, name, i), chunk) for i, chunk in enumerate(chunks)]

    def busy(self):
        return self.waiting or self.flights

    def step(self, main, count=WINDOW_STEP[0], steps=WINDOW_STEP[1]):
        self.now += 1
        landed = [flight for flight in self.flights if flight[0] <= self.now]
        self.flights = [flight for flight in self.flights if flight[0] > self.now]
        fresh, self.waiting = self.waiting[:count], self.waiting[count:]
        tied = (main, [flight[3:] for flight in landed], [item[1] for item in fresh])
        main, states, chunks = lax.optimization_barrier(tied)

        def launch(stage, key, value, axis, pairs, wait):
            got = lax.ppermute(value, axis, pairs)
            self.flights.append((self.now + wait, stage, key, value, got))

        for (_, stage, key, *_), (value, got) in zip(landed, states):
            if stage == 0:
                launch(1, key, add_low(value, got), DP, [(1, 2), (2, 1)], steps)
            elif stage == 1:
                launch(2, key, add_low(value, got), DP, [(1, 0), (2, 3)], steps)
            elif stage == 2:
                pair = (1, 0) if key[0] == 0 else (0, 1)
                launch(3, key, jnp.where(self.middle, value, got), SEC, [pair], 1)
            else:
                self.done[key] = (value, got)
        for (key, _), chunk in zip(fresh, chunks):
            launch(0, key, chunk, DP, [(0, 1), (3, 2)], steps)
        return main

    def result(self, section, name):
        keys = sorted(key for key in self.done if key[:2] == (section, name))
        return [self.done[key] for key in keys]


def cut(v, count):
    rows = v.shape[0] // count
    return [v[i * rows : (i + 1) * rows] for i in range(count)]


def to_heads(v, lanes, parts):
    tokens, columns = v.shape
    per = columns // (parts * lanes)
    split = v.reshape(tokens, parts, lanes, per).transpose(2, 0, 1, 3).reshape(lanes, tokens, parts * per)
    return a2a(split, DP).reshape(lanes * tokens, parts * per)


def to_tokens(v, lanes, parts):
    pack, columns = v.shape
    tokens, per = pack // lanes, columns // parts
    got = a2a(v.reshape(lanes, tokens, columns), DP).reshape(lanes, tokens, parts, per)
    return got.transpose(1, 2, 0, 3).reshape(tokens, lanes * columns)


def add_blocks(first, blocks):
    return functools.reduce(jnp.add, [block.astype(F32) for block in blocks], first)


def layer_mlp(middle, context, weights, beside=None):
    gain, w_small, w_sin, w_sdown, experts, which = weights
    me, slot, info, capacity, count = context
    members = slot.shape[0]
    hidden, scale = norm_apply(middle, gain)
    blocks = gather_blocks(hidden, members)
    out = moe_forward(which, slot, info, w_small, blocks, experts, w_sin, w_sdown, capacity, count)
    if beside is not None:
        out = beside(out)
    parts = scatter_blocks(out[9:])
    return add_blocks(middle, parts), (scale, hidden, blocks, *out[:9])


def mlp_backward(grad_blocks, middle, saved, context, weights, sums, ready, kernel_done):
    gain, w_small, w_sin, w_sdown, expert_weights, which = weights
    me, slot, info, capacity, experts = context
    scale, hidden, blocks, rows, gate, up, act, meta, ret, sg, su, sact = saved
    members, (tokens, width) = len(blocks), middle.shape
    out = moe_backward(
        which, slot, info, meta, grad_blocks, ret, expert_weights, gate, up, sg, su, w_sin, w_sdown
    )
    out = sums.step(kernel_done(out))
    dy, dg, du, dsg, dsu = out[:5]
    parts = scatter_blocks(out[5:])
    ready((rows, act, dy, dg, du), (blocks, sact, grad_blocks, dsg, dsu))
    parts = sums.step(parts)
    dh2 = add_blocks(jnp.zeros(middle.shape, F32), [part[:tokens] for part in parts])
    tails = [part[tokens : tokens + 2, :tokens].astype(F32) for part in parts]
    column = jnp.arange(experts, dtype=I32)[None, :]
    dgates = sum(
        jnp.where(column == (me ^ k), (tail[0] + tail[1])[:, None], 0.0) for k, tail in enumerate(tails)
    )
    router, chosen = meta[:tokens, :experts], info[:tokens, :experts]
    picked = jnp.sum(router * chosen, axis=-1, keepdims=True)
    inner = jnp.sum(dgates * router * chosen, axis=-1, keepdims=True) / picked
    dprob = chosen * (dgates - inner) / picked
    dlogits = (router * (dprob - jnp.sum(router * dprob, axis=-1, keepdims=True))).astype(BF)
    dh2 = dh2 + mm(dlogits, w_small[:, :experts], 1, 1)
    dmiddle_norm, dgain = norm_backward(dh2, middle, scale, gain)
    dmiddle = grad_blocks[0].astype(F32) + dmiddle_norm
    return dmiddle, dgain, dlogits


def halves(rows_of, grads, core):
    send = mm(half_of(rows_of, 1 - core, 1), grads, 0, 0, out=BF)
    keep = mm(half_of(rows_of, core, 1), grads, 0, 0)
    return (keep + swap_cores(send).astype(F32)).astype(BF)


def halves_by_member(rows_of, grads, core, members):
    split = rows_of.reshape(rows_of.shape[0], members, 2, -1)

    def side(which):
        return lax.dynamic_index_in_dim(split, which, 2, False).reshape(rows_of.shape[0], -1)

    send = mm(side(1 - core), grads, 0, 0, out=BF)
    keep = mm(side(core), grads, 0, 0)
    return (keep + swap_cores(send).astype(F32)).astype(BF).reshape(members, -1, grads.shape[1])


def expert_grads(terms, core):
    rows, act, dy, dg, du = terms
    g_in = jnp.concatenate([halves(rows, dg, core), halves(rows, du, core)], axis=1)
    return halves(act, dy, core), g_in


def shared_grads(terms, core):
    blocks, sact, grad_blocks, dsg, dsu = terms
    members = len(blocks)
    hidden_all, grad_all = jnp.concatenate(blocks), jnp.concatenate(grad_blocks)
    g_in = halves_by_member(hidden_all, jnp.concatenate([dsg, dsu], axis=1), core, members)
    return halves(sact, grad_all, core), a2a(g_in, EXP)


def dense_grads(terms, core, members):
    hidden_one, dqkv, mixed, dattn, hidden_two, dlogits, dgains = terms
    width, experts = hidden_one.shape[1], dlogits.shape[1]
    small = jnp.concatenate(
        [mm(hidden_two, dlogits, 0, 0), jnp.stack(dgains, axis=1), jnp.zeros((width, 126 - experts), F32)],
        axis=1,
    )
    split = small.reshape(members, 2, -1, 128)
    send = lax.dynamic_index_in_dim(split, 1 - core, 1, False).astype(BF)
    keep = lax.dynamic_index_in_dim(split, core, 1, False)
    small = (keep + swap_cores(send).astype(F32)).astype(BF)
    g_out = halves_by_member(mixed, dattn, core, members)
    g_qkv = halves_by_member(hidden_one, dqkv, core, members)
    return jnp.concatenate([g_qkv, g_out, small], axis=2)


def member_sum(parts):
    return jnp.sum(parts.astype(F32), axis=0).astype(BF)


def local(
    inputs, cotangent, lengths, deal, routes, order, gains, w_qkv, w_out, w_router, w_shared_in, w_shared_down,
    w_expert_in, w_expert_down,
):
    core, me = lax.axis_index(SEC), lax.axis_index(EXP)
    members, lanes = lax.axis_size(EXP), lax.axis_size(DP)
    batches, _, tokens, width = inputs.shape
    experts = w_router.shape[2]
    assert batches == lax.axis_size(SEC) == 2 and w_expert_in.shape[1] == 1 and experts == members
    w = Weights(
        core, members, gains[0], w_qkv[0], w_out[0], w_router[0], w_shared_in[0], w_shared_down[0],
        w_expert_in[0, 0], w_expert_down[0, 0],
    )
    first_low = lax.dynamic_index_in_dim(inputs[:, 0], core, 0, False)
    grad_low = lax.dynamic_index_in_dim(cotangent[:, 0], core, 0, False)
    row = lax.dynamic_index_in_dim(deal, core * members + me, 0, False)
    ends = jnp.cumsum(lax.dynamic_index_in_dim(lengths, row, 0, False))[:-1].astype(I32)
    qkv_0, w_small_0, gains_0 = w.split_first(w.both_halves(w.permuted(w.first_shares[0])))
    current_0 = first_low.astype(F32)
    hidden_0, scale_0 = norm_apply(current_0, gains_0[0])
    projected = mm(hidden_0, qkv_0, out=BF)
    pairs = lax.dynamic_index_in_dim(routes[:, 0], core, 0, False).reshape(-1)
    places = lax.dynamic_index_in_dim(order[:, 0], core, 0, False)
    same = pairs[:, None] == pairs[None, :]
    rank = jnp.sum((same & (places[None, :] < places[:, None])).astype(I32), axis=1)
    code = jnp.stack(gather_blocks(after(pairs * (2 * tokens) + rank, projected), members))
    owner = me ^ jnp.arange(members, dtype=I32)
    pairs_all, rank_all = code // (2 * tokens), code % (2 * tokens)
    onehot = (pairs_all[:, :, None] == jnp.arange(experts, dtype=I32)).astype(I32)
    counts = jnp.sum(onehot, axis=1)
    lower = (owner[None, :] < owner[:, None]).astype(I32)
    before = jnp.sum(lower[:, :, None] * counts[None], axis=1)
    place = jnp.sum(onehot * before[:, None, :], axis=2) + rank_all
    capacity = 2 * tokens * members // experts
    slot = jnp.where((pairs_all == me) & (place < capacity), place, -1)
    slot = jnp.max(slot.reshape(members, tokens, 2), axis=2)
    column = jnp.arange(128, dtype=I32)[None, :]
    named = pairs_all.reshape(members * tokens, 2)
    chosen = (named[:, :1] == column) | (named[:, 1:] == column)
    info = jnp.where(column == SPOT, slot.reshape(-1, 1).astype(F32), chosen.astype(F32))

    w_out_0 = w.both_halves(w.permuted(after(w.out_shares[0], projected)))
    shared_in = w.shared_in(after(w.w_sin, projected))
    shared = (shared_in, w.w_sdown)
    shared = (shared, (swap_cores(shared_in), swap_cores(w.w_sdown)))
    expert_weights = ((w.w_ein, w.w_edown), (swap_cores(w.w_ein), swap_cores(w.w_edown)))
    which = [jnp.stack([me, (core == s).astype(I32)]) for s in range(2)]
    heads_0 = to_heads(projected, lanes, 3)
    heads_0, slot, info = lax.optimization_barrier((heads_0, slot, info))
    context = (me, slot, info, capacity, experts)
    later = jnp.concatenate([w.first_shares[1], w.out_shares[1]], axis=1)
    mixed_0, shared = lax.optimization_barrier((attention_forward(ends, heads_0, tokens), shared))
    mixed_0 = to_tokens(mixed_0, lanes, 1)
    shared_first = [by_core(core, mine, other) for mine, other in zip(*shared)]
    mixed_0, shared_first = lax.optimization_barrier((mixed_0, shared_first))
    shared_second = [by_core(core, other, mine) for mine, other in zip(*shared)]
    middle_0 = current_0 + mm(mixed_0, w_out_0)
    gathered = []

    def land(out):
        out, full = lax.optimization_barrier((out, lax.all_gather(after(later, heads_0), EXP)))
        gathered.append(full)
        return out

    mlp_0 = (gains_0[1], w_small_0, *shared_first, expert_weights, which[0])
    out_0, saved_0 = layer_mlp(middle_0, context, mlp_0, land)
    dense_1 = w.both_halves(gathered[0])
    low_0, dense_1, shared_second = lax.optimization_barrier((out_0.astype(BF), dense_1, shared_second))
    qkv_1, w_small_1, gains_1 = w.split_first(dense_1)
    w_out_1 = dense_1[:, 3 * width + 128 :]
    current_1 = low_0.astype(F32)
    hidden_1, scale_1 = norm_apply(current_1, gains_1[0])
    projected = mm(hidden_1, qkv_1, out=BF)
    grad_blocks = gather_blocks(after(grad_low, projected), members)
    heads_1 = to_heads(projected, lanes, 3)
    heads_1, grad_blocks = lax.optimization_barrier((heads_1, grad_blocks))
    mixed_1 = to_tokens(attention_forward(ends, heads_1, tokens), lanes, 1)
    middle_1 = current_1 + mm(mixed_1, w_out_1)
    mlp_1 = (gains_1[1], w_small_1, *shared_second, expert_weights, which[1])
    out_1, saved_1 = layer_mlp(middle_1, context, mlp_1)
    low_1 = out_1.astype(BF)

    sums = LineSums()

    def backward(section, grad_blocks, current, hidden, scale, heads, mixed, middle, saved, gain, w_qkv_s, w_out_s, mlp, beside=None):
        shared = []

        def kernel_done(out):
            if beside is None:
                return out
            out, parts = lax.optimization_barrier((out, a2a(beside, EXP)))
            sums.add(1 - section, 4, [member_sum(parts)])
            return out

        def ready(terms, shared_terms):
            down, ein = expert_grads(terms, core)
            sums.add(section, 0, cut(down, CHUNKS[0]))
            sums.add(section, 1, cut(ein, CHUNKS[1]))
            shared.append(shared_terms)

        dmiddle, dgain_two, dlogits = mlp_backward(
            grad_blocks, middle, saved, context, mlp, sums, ready, kernel_done
        )
        dattn = dmiddle.astype(BF)
        dheads = to_heads(mm(dattn, w_out_s, 1, 1, out=BF), lanes, 1)
        g_sdown, g_sin = shared_grads(shared[0], core)
        sums.add(section, 2, [g_sdown])
        sums.add(section, 3, [g_sin.reshape(-1, g_sin.shape[2])])
        dheads = sums.step(dheads)
        dheads = sums.step(attention_backward(ends, heads, dheads, tokens))
        dqkv = sums.step(to_tokens(dheads, lanes, 3))
        dinput, dgain_one = norm_backward(mm(dqkv, w_qkv_s, 1, 1), current, scale, gain)
        dense = (hidden, dqkv, mixed, dattn, saved[1], dlogits, (dgain_one, dgain_two))
        return dmiddle + dinput, dense_grads(dense, core, members)

    grad_1, dense_1 = backward(
        1, grad_blocks, current_1, hidden_1, scale_1, heads_1, mixed_1, middle_1, saved_1, gains_1[0], qkv_1,
        w_out_1, mlp_1,
    )
    grad_blocks, dense_1 = lax.optimization_barrier((gather_blocks(grad_1.astype(BF), members), dense_1))
    grad_blocks = sums.step(grad_blocks)
    grad_0, dense_0 = backward(
        0, grad_blocks, current_0, hidden_0, scale_0, heads_0, mixed_0, middle_0, saved_0, gains_0[0], qkv_0,
        w_out_0, mlp_0, dense_1,
    )
    sums.add(0, 4, [member_sum(a2a(dense_0, EXP))])
    quarter = FF // members

    def by_columns(half):
        blocks = half.reshape(members, -1, 2 * quarter)
        return jnp.concatenate(
            [blocks[j][:, at : at + quarter] for at in (0, quarter) for j in range(members)], axis=1
        )

    def whole(name):
        own_0, got_0 = zip(*sums.result(0, name))
        own_1, got_1 = zip(*sums.result(1, name))
        pairs = zip(own_0 + got_0, got_1 + own_1)
        parts = [by_core(core, a, b) for a, b in pairs]
        return jnp.concatenate([by_columns(v) if name == 3 else v for v in parts]).astype(F32)

    def complete(name):
        return all(len(sums.result(section, name)) == CHUNKS[name] for section in range(2))

    results = {}
    while sums.busy():
        results = sums.step(results, *TAIL_STEP)
        results.update({name: whole(name) for name in range(5) if name not in results and complete(name)})

    def to_section(of_0, of_1):
        mine = by_core(core, of_0, of_1)
        other = swap_cores(by_core(core, of_1, of_0))
        both = jnp.stack([by_core(core, mine, other), by_core(core, other, mine)])
        return both[None, :, None]

    down, ein, sdown, sin, dense = [results[name] for name in range(5)]
    at = 4 * width
    return (
        to_section(low_0, low_1),
        to_section(grad_0, grad_1),
        dense[:, at + experts : at + experts + 2].T[None],
        dense[None, :, : 3 * width],
        dense[None, :, 3 * width : at],
        dense[None, :, at : at + experts],
        sin[None],
        sdown[None],
        ein[None, None],
        down[None, None],
    )


def solution(mesh):
    tokens = P(None, EXP, DP, None)
    dense = P(SEC, EXP, None)
    expert = P(SEC, EXP, None, None)
    both = P(SEC, None, EXP, DP, None)
    gains = P(SEC, None, EXP)
    return jax.shard_map(
        local,
        mesh=mesh,
        in_specs=(tokens, tokens, P(), P(), tokens, P(None, EXP, DP), gains)
        + (dense,) * 5
        + (expert,) * 2,
        out_specs=(both, both, gains) + (dense,) * 5 + (expert,) * 2,
        check_vma=False,
    )
```
